32 devices in a mesh: owner: 4 (over y, core), dp: 8 (over z, x).
Axes of the slice: x: 2, y: 2, z: 4, core: 2. Of those that a mesh axis runs over, the one named last changes fastest.
Arguments:
- activations: bfloat16 [64, 8, 8, 512], P(('owner', 'dp')), may hold values from -8 to 8
- out_grad: bfloat16 [64, 8, 8, 512], P(('owner', 'dp')), may hold values from -6 to 6
- group_weight: bfloat16 [16, 288, 32], replicated, may hold values from -0.375 to 0.375
- proj_weight: bfloat16 [512, 512], replicated, may hold values from -0.25 to 0.25
- bn_gain: float32 [512], replicated, may hold values from 0.1 to 1.9
- bn_shift: float32 [512], replicated, may hold values from -3 to 3
- slot_block: int32 [4, 24], replicated, may hold values from -1 to 47, as said below
Outputs:
- group_grad: float32 [16, 288, 32], replicated
- proj_grad: float32 [512, 512], replicated
- out_factor: float32 [16, 32, 32], replicated
- factor_owned: float32 [96, 96, 288], P('owner', 'dp')
The draws below stay inside these ranges and needn't reach their ends.
Inputs may be any that keep to these rules, and one draw needn't show every extreme that they name: `slot_block`: each of the 48 blocks stands in exactly one slot; an owner's blocks fill its slots from the first, the rest hold -1; some owner's 24 slots are all used.
All inputs are finite; a program needn't handle non-finite values.
Results may differ from the reference program's by a relative error of at most 0.0065.
Values sent between devices are 32-bit elements; how exact they have to be, the bound alone decides.
No kernel may reach another device: no remote copies, remote signals or barrier semaphores. Data moves between devices by JAX's collectives and lax.ppermute only.
A program may use at most 64 MiB of HBM per device.

```python
import math
import jax
import jax.numpy as jnp
from jax import lax

GRP = 16
GW = 32
COUT = 512
SIDE = 8
IMG_DEV = 2
CIN = 512
CPATCH = 288
BROWS = 96
NB = 48
SLOTS = 24
IMGS = 64
ROWS = 4096
N_OWNER = 4
N_DP = 8


def draw_activations(key, part):
    key_base, key_image, key_channel = jax.random.split(key, 3)
    shape = (IMGS, SIDE, SIDE, CIN)
    base = jax.random.normal(key_base, shape, jnp.float32)
    mixed = base + 0.7 * jnp.roll(base, 1, axis=3) + 0.5 * jnp.roll(base, 1, axis=2)
    image_scale = jnp.exp(0.7 * jax.random.uniform(key_image, (IMGS, 1, 1, 1), jnp.float32, -1.0, 1.0))
    channel_scale = jnp.exp(0.5 * jax.random.uniform(key_channel, (CIN,), jnp.float32, -1.0, 1.0))
    values = 0.6 * mixed * image_scale * channel_scale
    return jnp.clip(values, -8.0, 8.0).astype(jnp.bfloat16)


def draw_slot_block(key, part):
    key_order, key_busy = jax.random.split(key)
    block_order = jax.random.permutation(key_order, NB).astype(jnp.int32)
    busiest = jax.random.randint(key_busy, (), 0, N_OWNER)
    position = jnp.arange(NB, dtype=jnp.int32)
    beyond = jnp.maximum(position - SLOTS, 0)
    others = N_OWNER - 1
    owner_index = jnp.where(position < SLOTS, busiest, (busiest + 1 + beyond % others) % N_OWNER)
    slot_index = jnp.where(position < SLOTS, position, beyond // others)
    slot_table = jnp.full((N_OWNER, SLOTS), -1, jnp.int32)
    return slot_table.at[owner_index, slot_index].set(block_order)


def level_of(own_key, dims, shards, low, high):
    def one(axis_at, parts):
        draws = jax.random.uniform(jax.random.fold_in(jax.random.fold_in(own_key, 6), axis_at), (parts,), jnp.float32, low / len(shards), high / len(shards))
        return jnp.repeat(jnp.exp(draws), dims[axis_at] // parts).reshape((-1,) + (1,) * (len(dims) - axis_at - 1))

    loudness = one(*shards[0])
    for cut in shards[1:]:
        loudness = loudness * one(*cut)
    return loudness


def gaussian(key, shape, spread, reach, cuts=(), kind=jnp.bfloat16):
    array = jax.random.normal(key, shape, jnp.float32) * spread
    if len(cuts) > 0:
        array = level_of(key, shape, cuts, -0.22, 0.18) * array
    return jnp.clip(array, min=-reach, max=reach).astype(kind)


def setup_inputs(seed: int = 0) -> dict:
    keys = jax.random.split(jax.random.key(seed), 8)
    activations = draw_activations(jax.random.fold_in(keys[7], 71), 0)
    out_grad = gaussian(keys[1], (IMGS, SIDE, SIDE, COUT), 1.0, 6.0, ((0, 32),))
    group_weight = gaussian(keys[2], (GRP, CPATCH, GW), CPATCH ** -0.5, 0.375)
    proj_weight = gaussian(keys[3], (CIN, COUT), CIN ** -0.5, 0.25)
    bn_gain = jnp.clip(1.0 + 0.18 * jax.random.normal(keys[4], (CIN,), jnp.float32), 0.1, 1.9)
    bn_shift = gaussian(keys[5], (CIN,), 0.5, 3.0, (), jnp.float32)
    slot_block = draw_slot_block(jax.random.fold_in(keys[7], 71), 0)
    return dict(activations=activations, out_grad=out_grad, group_weight=group_weight, proj_weight=proj_weight, bn_gain=bn_gain, bn_shift=bn_shift, slot_block=slot_block)


def patch_rows(images):
    count = images.shape[0]
    padded = jnp.pad(images, ((0, 0), (1, 1), (1, 1), (0, 0)))
    padded = padded.reshape(count, SIDE + 2, SIDE + 2, GRP, GW)
    shifted = [padded[:, row_shift:row_shift + SIDE, col_shift:col_shift + SIDE] for row_shift in range(3) for col_shift in range(3)]
    return jnp.stack(shifted, axis=4).reshape(count * SIDE * SIDE, GRP, 9 * GW)

def reference(activations, out_grad, group_weight, proj_weight, bn_gain, bn_shift, slot_block):
    blocks_count = N_OWNER * N_DP
    act_blocks = activations.reshape(blocks_count, IMG_DEV, SIDE, SIDE, CIN)
    grad_blocks = out_grad.reshape(blocks_count, IMG_DEV * SIDE * SIDE, COUT)
    weight_full = group_weight.astype(jnp.float32)
    proj_full = proj_weight.astype(jnp.float32)

    def accumulate(carry, pieces):
        group_sum, proj_sum, out_sum, in_sum = carry
        images, upstream = pieces
        patches = patch_rows(images).astype(jnp.float32)
        conv_out = jnp.einsum('rgp,gpo->rgo', patches, weight_full).reshape(-1, CIN)
        preact = conv_out * bn_gain + bn_shift
        hidden = jnp.maximum(preact, 0.0).astype(jnp.bfloat16)
        upstream_full = upstream.astype(jnp.float32)
        back_grad = jnp.einsum('ro,co->rc', upstream_full, proj_full)
        grad_pre = jnp.where(preact > 0.0, back_grad * bn_gain, 0.0).astype(jnp.bfloat16)
        grad_pre = lax.optimization_barrier(grad_pre)
        grad_full = grad_pre.astype(jnp.float32).reshape(-1, GRP, GW)
        hidden_full = hidden.astype(jnp.float32)
        group_sum = group_sum + jnp.einsum('rgp,rgo->gpo', patches, grad_full)
        proj_sum = proj_sum + jnp.einsum('rc,ro->co', hidden_full, upstream_full)
        out_sum = out_sum + jnp.einsum('rga,rgb->gab', grad_full, grad_full)
        in_sum = in_sum + jnp.einsum('rgp,rgq->gpq', patches, patches)
        return ((group_sum, proj_sum, out_sum, in_sum), None)
    start = (jnp.zeros((GRP, CPATCH, GW), jnp.float32), jnp.zeros((CIN, COUT), jnp.float32), jnp.zeros((GRP, GW, GW), jnp.float32), jnp.zeros((GRP, CPATCH, CPATCH), jnp.float32))
    sums, _ = lax.scan(accumulate, start, (act_blocks, grad_blocks))
    group_sum, proj_sum, out_sum, in_sum = sums
    grad_scale = 1.0 / math.sqrt(ROWS)
    mean_scale = 1.0 / ROWS
    factor_blocks = in_sum.reshape(NB, BROWS, CPATCH)
    flat_slots = slot_block.reshape(-1)
    picked = jnp.take(factor_blocks, jnp.clip(flat_slots, 0, NB - 1), axis=0)
    live = (flat_slots >= 0).astype(jnp.float32)
    factor_owned = picked * live[:, None, None] * mean_scale
    return (group_sum * grad_scale, proj_sum * grad_scale, out_sum * mean_scale, factor_owned)
```

```python
import functools
import math

import jax
import jax.numpy as jnp
from jax import lax
from jax.experimental import pallas as pl
from jax.experimental.pallas import tpu as pltpu
from jax.sharding import PartitionSpec as P

AXES = ("owner", "dp")
F32 = jnp.float32
BF16 = jnp.bfloat16
VMEM_LIMIT = 48 * 1024 * 1024
PAIRS = ((0, 0), (0, 1), (0, 2), (1, 0), (1, 1), (2, 0), (2, 2))
SAME = {(1, 2): (0, 1), (2, 1): (1, 0)}


def whole_vmem():
    return pl.BlockSpec(memory_space=pltpu.VMEM)


def call(body, outs, scratch, *args):
    return pl.pallas_call(
        body,
        out_shape=[jax.ShapeDtypeStruct(shape, kind) for shape, kind in outs],
        in_specs=[whole_vmem() if a.dtype != jnp.int32 else pl.BlockSpec(memory_space=pltpu.SMEM) for a in args],
        out_specs=[whole_vmem() for _ in outs],
        scratch_shapes=scratch,
        compiler_params=pltpu.CompilerParams(vmem_limit_bytes=VMEM_LIMIT),
    )(*args)


def plane_id():
    owner, dp = lax.axis_index("owner"), lax.axis_index("dp")
    return (owner & 1) * 4 + ((owner >> 1) & 1) * 2 + (dp & 1)


def cell_id():
    return plane_id() * 4 + ((lax.axis_index("dp") >> 1) & 3)


def send_kernel(x_ref, *refs):
    out_refs, held = refs[:-1], refs[-1]
    me = plane_id()
    x_t = x_ref[...].astype(F32).reshape(128, 512).T
    for block in range(8):
        held[block ^ me] = x_t[64 * block : 64 * block + 64]
    for place, out in enumerate(out_refs):
        out[...] = held[place]


def shift_rows(value, row_step, col_step):
    images, side, _, width = value.shape
    if col_step != 0:
        flat = value.reshape(images * side, side, width)
        flat = pltpu.roll(flat, (-col_step) % side, 1)
        column = lax.broadcasted_iota(jnp.int32, flat.shape, 1) + col_step
        value = jnp.where((column >= 0) & (column < side), flat, 0.0).reshape(value.shape)
    if row_step != 0:
        edge = jnp.zeros((images, 1, side, width), F32)
        if row_step < 0:
            value = jnp.concatenate([edge, value[:, :-1]], axis=1)
        else:
            value = jnp.concatenate([value[:, 1:], edge], axis=1)
    return value


def diagonal(square):
    lane = lax.broadcasted_iota(jnp.int32, (32, 128), 1)
    out = square[96:128]
    for g in (2, 1, 0):
        out = jnp.where(lane < 32 * (g + 1), square[32 * g : 32 * g + 32], out)
    return out


def local_kernel(x_ref, og_ref, gw_ref, pw_ref, gain_ref, shift_ref, mine_ref, other_ref, block_w, hid_t, sums):
    me = cell_id()
    images = x_ref.shape[0]
    rows = images * 64
    spot_row = lax.broadcasted_iota(jnp.int32, (32, 128), 0)
    spot_lane = lax.broadcasted_iota(jnp.int32, (32, 128), 1)
    for g in range(16):
        place = (spot_lane == spot_row + 32 * (g % 4)).astype(F32).astype(BF16)
        spread = jnp.dot(gw_ref[g], place, preferred_element_type=F32).astype(BF16)
        for s in range(9):
            at = s * 128 + 32 * (g % 4)
            block_w[g // 4, at : at + 32, :] = spread[32 * s : 32 * s + 32]
    x = x_ref[...].astype(F32)
    moved = [
        shift_rows(x, a - 1, b - 1).reshape(rows, 512).astype(BF16) for a in range(3) for b in range(3)
    ]
    conv = []
    for q in range(4):
        lhs = jnp.concatenate([m[:, 128 * q : 128 * q + 128] for m in moved], axis=1)
        conv.append(jnp.dot(lhs, block_w[q], preferred_element_type=F32))
    conv = jnp.concatenate(conv, axis=1)
    gain = gain_ref[...]
    preact = conv * gain + shift_ref[...]
    hidden = jnp.maximum(preact, 0.0)
    og = og_ref[...].reshape(rows, 512)
    back = lax.dot_general(og, pw_ref[...], (((1,), (1,)), ((), ())), preferred_element_type=F32)
    grad = jnp.where(preact > 0.0, back * gain, 0.0).astype(BF16).astype(F32)
    h_t = hidden.T.astype(BF16)
    for j in range(32):
        hid_t[j ^ me] = h_t[16 * j : 16 * j + 16]
    for half, out in enumerate((mine_ref, other_ref)):
        lhs = hid_t[16 * half : 16 * half + 16].reshape(256, rows)
        part = jnp.dot(lhs, og, preferred_element_type=F32)
        for k in range(16):
            for w in range(4):
                out[k, 16 * w : 16 * w + 16, :] = part[16 * k : 16 * k + 16, 128 * w : 128 * w + 128]
    x_t = x.reshape(rows, 512).T.astype(BF16)
    g_t = grad.reshape(rows, 512).T.astype(BF16)
    grad4 = grad.reshape(images, 8, 8, 512)
    back_moved = [
        shift_rows(grad4, 1 - a, 1 - b).reshape(rows, 512).astype(BF16) for a in range(3) for b in range(3)
    ]
    for q in range(4):
        cut = slice(128 * q, 128 * q + 128)
        rhs = jnp.concatenate([m[:, cut] for m in back_moved], axis=1)
        part = jnp.dot(x_t[cut], rhs, preferred_element_type=F32)
        for s in range(9):
            at = 320 * q + 32 * s
            sums[at : at + 32, :] = diagonal(part[:, 128 * s : 128 * s + 128])
        part = jnp.dot(g_t[cut], back_moved[4][:, cut], preferred_element_type=F32)
        sums[320 * q + 288 : 320 * q + 320, :] = diagonal(part)
    for half, out in enumerate((mine_ref, other_ref)):
        for k in range(16):
            j = (16 * half + k) ^ me
            out[k, 64:104, :] = sums[pl.ds(pl.multiple_of(40 * j, 8), 40), :]


def factor_kernel(steps, *refs):
    parts, outs, (patches, held) = refs[:8], refs[8 : 8 + steps], refs[8 + steps :]
    me = lax.axis_index("dp") >> 1
    lane = lax.broadcasted_iota(jnp.int32, (64, 128), 1)
    row, col = (lane >> 3) & 7, lane & 7
    for src, ref in enumerate(parts):
        x_t = ref[...]
        for a in range(3):
            for b in range(3):
                step = (a - 1) * 8 + b - 1
                value = x_t if step == 0 else pltpu.roll(x_t, (-step) % 128, 1)
                keep = (row + a >= 1) & (row + a <= 8) & (col + b >= 1) & (col + b <= 8)
                value = jnp.where(keep, value, 0.0).astype(BF16)
                at = (3 * a + b) * 32
                patches[0, at : at + 32, 128 * src : 128 * src + 128] = value[:32]
                patches[1, at : at + 32, 128 * src : 128 * src + 128] = value[32:]
    pieces = []
    for g in range(2):
        for a, width in ((0, 288), (1, 192), (2, 288)):
            part = lax.dot_general(
                patches[g, 96 * a : 96 * a + 96, :],
                patches[g, :width, :],
                (((1,), (1,)), ((), ())),
                preferred_element_type=F32,
            )
            for pair in PAIRS:
                if pair[0] == a:
                    pieces.append(part[:, 96 * pair[1] : 96 * pair[1] + 96])
    full = jnp.concatenate(pieces, axis=1)
    size = 96 // steps
    for t in range(steps):
        held[t ^ me] = full[size * t : size * t + size]
    for t, out in enumerate(outs):
        out[...] = held[t]


def slots_kernel(scale, groups_of, slot_ref, *refs):
    parts, out_ref, held = refs[:8], refs[8], refs[9]
    me = plane_id()
    for place, ref in enumerate(parts):
        value = ref[...] * scale
        for g in range(2):
            for a in range(3):
                pieces = []
                for b in range(3):
                    at = 672 * g + 96 * PAIRS.index(SAME.get((a, b), (a, b)))
                    pieces.append(value[:, at : at + 96])
                held[6 * (place ^ me) + 3 * g + a] = jnp.concatenate(pieces, axis=1)
    owner = lax.axis_index("owner")
    for s in range(out_ref.shape[0]):
        block = slot_ref[owner, s]
        value = held[jnp.maximum(block, 0)]
        out_ref[s] = jnp.where(block >= 0, value, 0.0)


def unpack_kernel(grad_scale, mean_scale, *refs):
    parts, (group_ref, proj_ref, out_ref), sums = refs[:8], refs[8:11], refs[11]
    me = cell_id()
    for place, ref in enumerate(parts):
        for z in range(4):
            j = (4 * place + z) ^ me
            for w in range(4):
                at = pl.multiple_of(16 * j, 16)
                proj_ref[pl.ds(at, 16), 128 * w : 128 * w + 128] = ref[z, 16 * w : 16 * w + 16, :] * grad_scale
            sums[pl.ds(pl.multiple_of(40 * j, 8), 40), :] = ref[z, 64:104, :]
    for g in range(16):
        base, lanes = 320 * (g // 4), slice(32 * (g % 4), 32 * (g % 4) + 32)
        group_ref[g] = sums[base : base + 288, lanes] * grad_scale
        out_ref[g] = sums[base + 288 : base + 320, lanes] * mean_scale


def per_device(n_owner, n_dp, activations, out_grad, group_weight, proj_weight, bn_gain, bn_shift, slot_block):
    def swap(value, owner_mask, dp_mask):
        pairs = [
            (o * n_dp + d, (o ^ owner_mask) * n_dp + (d ^ dp_mask)) for o in range(n_owner) for d in range(n_dp)
        ]
        return lax.ppermute(value, AXES, pairs)

    def add_over(value, owner_bits, dp_bits):
        for bit in owner_bits:
            value = value + swap(value, 1 << bit, 0)
        for bit in dp_bits:
            value = value + swap(value, 0, 1 << bit)
        return value

    far_owner = range(2, n_owner.bit_length() - 1)
    far_dp = range(3, n_dp.bit_length() - 1)
    steps = n_dp // 2
    images = activations.shape[0]
    rows = images * 64
    total_rows = rows * n_owner * n_dp
    grad_scale = 1.0 / math.sqrt(total_rows)
    mean_scale = 1.0 / total_rows

    sent = call(send_kernel, [((64, 128), F32)] * 8, [pltpu.VMEM((8, 64, 128), F32)], activations)
    owner_of = lambda p: ((p >> 2) & 1) | (p & 2)
    got = [sent[0]] + [swap(sent[p], owner_of(p), p & 1) for p in range(1, 8)]

    mine, other = call(
        local_kernel,
        [((16, 104, 128), F32)] * 2,
        [
            pltpu.VMEM((4, 1152, 128), BF16),
            pltpu.VMEM((32, 16, rows), BF16),
            pltpu.VMEM((1280, 128), F32),
        ],
        activations,
        out_grad,
        group_weight,
        proj_weight,
        bn_gain.reshape(1, -1),
        bn_shift.reshape(1, -1),
    )
    total = mine + swap(other, 1, 0)
    total = total[0:4] + swap(total[4:8], 0, 1) + swap(total[8:12], 2, 0) + swap(total[12:16], 2, 1)
    total = total[0] + swap(total[1], 0, 2) + swap(total[2], 0, 4) + swap(total[3], 0, 6)
    total = add_over(total, far_owner, far_dp)
    total = jnp.stack([total] + [swap(total, 0, 2 * z) for z in range(1, 4)])
    near = [total] + [swap(total, 2 * (p >> 1), p & 1) for p in range(1, 4)]
    parts = near + [swap(v, 1, 0) for v in near]
    group_grad, proj_grad, out_factor = call(
        functools.partial(unpack_kernel, grad_scale, mean_scale),
        [((16, 288, 32), F32), ((512, 512), F32), ((16, 32, 32), F32)],
        [pltpu.VMEM((1280, 128), F32)],
        *parts,
    )

    size = 96 // steps
    pieces = call(
        functools.partial(factor_kernel, steps),
        [((size, 1344), F32)] * steps,
        [pltpu.VMEM((2, 288, 1024), BF16), pltpu.VMEM((steps, size, 1344), F32)],
        *got,
    )
    piece = pieces[0]
    for t in range(1, steps):
        piece = piece + swap(pieces[t], 0, 2 * t)
    piece = add_over(piece, far_owner, ())
    half = size // 2
    at = (lax.axis_index("dp") & 1) * half
    own = lax.dynamic_slice_in_dim(piece, at, half, 0)
    peer = lax.dynamic_slice_in_dim(piece, half - at, half, 0)
    near = [own, swap(peer, 0, 1), swap(own, 2, 0), swap(peer, 2, 1)]
    parts = near + [swap(v, 1, 0) for v in near]
    slots = slot_block.shape[1]
    (factor_owned,) = call(
        functools.partial(slots_kernel, mean_scale, 2),
        [((slots, half, 288), F32)],
        [pltpu.VMEM((48, half, 288), F32)],
        slot_block,
        *parts,
    )
    return group_grad, proj_grad, out_factor, factor_owned


def solution(mesh):
    placed = (P(AXES, None, None, None), P(AXES, None, None, None), P(), P(), P(), P(), P())
    return jax.shard_map(
        functools.partial(per_device, mesh.shape["owner"], mesh.shape["dp"]),
        mesh=mesh,
        in_specs=placed,
        out_specs=(P(), P(), P(), P("owner", "dp", None)),
        check_vma=False,
    )
```

```python
import functools
import math

import jax
import jax.numpy as jnp
from jax import lax
from jax.experimental import pallas as pl
from jax.experimental.pallas import tpu as pltpu
from jax.sharding import PartitionSpec as P

AXES = ("owner", "dp")
F32 = jnp.float32
BF16 = jnp.bfloat16
VMEM_LIMIT = 48 * 1024 * 1024
PAIRS = ((0, 0), (0, 1), (0, 2), (1, 0), (1, 1), (2, 0), (2, 2))
SAME = {(1, 2): (0, 1), (2, 1): (1, 0)}


def whole_vmem():
    return pl.BlockSpec(memory_space=pltpu.VMEM)


def call(body, outs, scratch, *args, in_hbm=False):
    def place(arg):
        if arg.dtype == jnp.int32:
            return pl.BlockSpec(memory_space=pltpu.SMEM)
        return pl.BlockSpec(memory_space=pltpu.HBM) if in_hbm else whole_vmem()

    return pl.pallas_call(
        body,
        out_shape=[jax.ShapeDtypeStruct(shape, kind) for shape, kind in outs],
        in_specs=[place(a) for a in args],
        out_specs=[whole_vmem() for _ in outs],
        scratch_shapes=scratch,
        compiler_params=pltpu.CompilerParams(vmem_limit_bytes=VMEM_LIMIT),
    )(*args)


def plane_id():
    owner, dp = lax.axis_index("owner"), lax.axis_index("dp")
    return (owner & 1) * 4 + ((owner >> 1) & 1) * 2 + (dp & 1)


def cell_id():
    return plane_id() * 4 + ((lax.axis_index("dp") >> 1) & 3)


def send_kernel(x_hbm, keep_ref, give_ref, x_ref, held, sem):
    copy = pltpu.make_async_copy(x_hbm, x_ref, sem)
    copy.start()
    me = plane_id()
    copy.wait()
    x_t = x_ref[...].astype(F32).reshape(128, 512).T
    for block in range(8):
        held[block ^ me] = x_t[64 * block : 64 * block + 64]
    keep_ref[...] = held[0:4]
    give_ref[...] = held[4:8]


def shift_rows(value, row_step, col_step):
    images, side, _, width = value.shape
    if col_step != 0:
        flat = value.reshape(images * side, side, width)
        flat = pltpu.roll(flat, (-col_step) % side, 1)
        column = lax.broadcasted_iota(jnp.int32, flat.shape, 1) + col_step
        value = jnp.where((column >= 0) & (column < side), flat, 0.0).reshape(value.shape)
    if row_step != 0:
        edge = jnp.zeros((images, 1, side, width), F32)
        if row_step < 0:
            value = jnp.concatenate([edge, value[:, :-1]], axis=1)
        else:
            value = jnp.concatenate([value[:, 1:], edge], axis=1)
    return value


def diagonal(square):
    lane = lax.broadcasted_iota(jnp.int32, (32, 128), 1)
    out = square[96:128]
    for g in (2, 1, 0):
        out = jnp.where(lane < 32 * (g + 1), square[32 * g : 32 * g + 32], out)
    return out


def local_kernel(*refs):
    sources, (mine_ref, other_ref), held, sems = refs[:6], refs[6:8], refs[8:14], refs[14]
    block_w, hid_t, sums = refs[15:]
    copies = [pltpu.make_async_copy(src, dst, sems.at[i]) for i, (src, dst) in enumerate(zip(sources, held))]
    for copy in copies:
        copy.start()
    x_ref, og_ref, gw_ref, pw_ref, gain_ref, shift_ref = held
    me = cell_id()
    images = x_ref.shape[0]
    rows = images * 64
    for copy in copies:
        copy.wait()
    group_at = lax.broadcasted_iota(jnp.int32, (32, 128), 1) // 32
    for q in range(4):
        stacked = gw_ref[4 * q : 4 * q + 4].astype(F32).reshape(128, 288).T
        for s in range(9):
            for g in range(4):
                at = s * 128 + 32 * g
                block_w[q, at : at + 32, :] = jnp.where(group_at == g, stacked[32 * s : 32 * s + 32], 0.0).astype(BF16)
    x = x_ref[...].astype(F32)
    moved = [
        shift_rows(x, a - 1, b - 1).reshape(rows, 512).astype(BF16) for a in range(3) for b in range(3)
    ]
    conv = []
    for q in range(4):
        lhs = jnp.concatenate([m[:, 128 * q : 128 * q + 128] for m in moved], axis=1)
        conv.append(jnp.dot(lhs, block_w[q], preferred_element_type=F32))
    conv = jnp.concatenate(conv, axis=1)
    gain = gain_ref[...]
    preact = conv * gain + shift_ref[...]
    hidden = jnp.maximum(preact, 0.0)
    og = og_ref[...].reshape(rows, 512)
    back = lax.dot_general(og, pw_ref[...], (((1,), (1,)), ((), ())), preferred_element_type=F32)
    grad = jnp.where(preact > 0.0, back * gain, 0.0).astype(BF16).astype(F32)
    h_t = hidden.T.astype(BF16)
    for j in range(32):
        hid_t[j ^ me] = h_t[16 * j : 16 * j + 16]
    for half, out in enumerate((mine_ref, other_ref)):
        lhs = hid_t[16 * half : 16 * half + 16].reshape(256, rows)
        part = jnp.dot(lhs, og, preferred_element_type=F32)
        for k in range(16):
            for w in range(4):
                out[k, 16 * w : 16 * w + 16, :] = part[16 * k : 16 * k + 16, 128 * w : 128 * w + 128]
    x_t = x.reshape(rows, 512).T.astype(BF16)
    g_t = grad.reshape(rows, 512).T.astype(BF16)
    grad4 = grad.reshape(images, 8, 8, 512)
    back_moved = [
        shift_rows(grad4, 1 - a, 1 - b).reshape(rows, 512).astype(BF16) for a in range(3) for b in range(3)
    ]
    for q in range(4):
        cut = slice(128 * q, 128 * q + 128)
        rhs = jnp.concatenate([m[:, cut] for m in back_moved], axis=1)
        part = jnp.dot(x_t[cut], rhs, preferred_element_type=F32)
        for s in range(9):
            at = 320 * q + 32 * s
            sums[at : at + 32, :] = diagonal(part[:, 128 * s : 128 * s + 128])
        part = jnp.dot(g_t[cut], back_moved[4][:, cut], preferred_element_type=F32)
        sums[320 * q + 288 : 320 * q + 320, :] = diagonal(part)
    for half, out in enumerate((mine_ref, other_ref)):
        for k in range(16):
            j = (16 * half + k) ^ me
            out[k, 64:104, :] = sums[pl.ds(pl.multiple_of(40 * j, 8), 40), :]


def factor_kernel(steps, *refs):
    parts, outs, (patches, held) = refs[:5], refs[5 : 5 + steps], refs[5 + steps :]
    dp = lax.axis_index("dp")
    lane = lax.broadcasted_iota(jnp.int32, (64, 128), 1)
    row, col = (lane >> 3) & 7, lane & 7
    sources = [parts[0][0], parts[1][0]] + [ref[i] for ref in parts[2:] for i in range(2)]
    for src, x_t in enumerate(sources):
        for a in range(3):
            for b in range(3):
                step = (a - 1) * 8 + b - 1
                value = x_t if step == 0 else pltpu.roll(x_t, (-step) % 128, 1)
                keep = (row + a >= 1) & (row + a <= 8) & (col + b >= 1) & (col + b <= 8)
                value = jnp.where(keep, value, 0.0).astype(BF16)
                at = (3 * a + b) * 32
                patches[0, at : at + 32, 128 * src : 128 * src + 128] = value[:32]
                patches[1, at : at + 32, 128 * src : 128 * src + 128] = value[32:]
    pieces = []
    for g in range(2):
        for a, width in ((0, 288), (1, 192), (2, 288)):
            part = lax.dot_general(
                patches[g, 96 * a : 96 * a + 96, :],
                patches[g, :width, :],
                (((1,), (1,)), ((), ())),
                preferred_element_type=F32,
            )
            for pair in PAIRS:
                if pair[0] == a:
                    pieces.append(part[:, 96 * pair[1] : 96 * pair[1] + 96])
    pieces.append(jnp.zeros((96, 64), F32))
    full = jnp.concatenate(pieces, axis=1)
    half = 96 // (2 * steps)
    for t in range(2 * steps):
        for tile in range(11):
            held[t ^ dp, half * tile : half * tile + half, :] = full[
                half * t : half * t + half, 128 * tile : 128 * tile + 128
            ]
        if 11 * half < held.shape[1]:
            held[t ^ dp, 11 * half :, :] = jnp.zeros((held.shape[1] - 11 * half, 128), F32)
    for t, out in enumerate(outs):
        out[...] = held[2 * t : 2 * t + 2]


def finish_kernel(grad_scale, mean_scale, slot_ref, *refs):
    parts, (group_ref, proj_ref, out_ref, owned_ref), (sums, blocks) = refs[:8], refs[8:12], refs[12:]
    me, plane = cell_id(), plane_id()
    half = owned_ref.shape[0]
    for place, ref in enumerate(parts):
        for z in range(4):
            j = (4 * place + z) ^ me
            for w in range(4):
                at = pl.multiple_of(16 * j, 16)
                row = 104 * z + 16 * w
                proj_ref[pl.ds(at, 16), 128 * w : 128 * w + 128] = ref[row : row + 16, :] * grad_scale
            sums[pl.ds(pl.multiple_of(40 * j, 8), 40), :] = ref[104 * z + 64 : 104 * z + 104, :]
        tiles = [ref[416 + half * t : 416 + half * t + half, :] for t in range(11)]
        value = jnp.concatenate(tiles, axis=1) * mean_scale
        for g in range(2):
            for a in range(3):
                pieces = []
                for b in range(3):
                    at = 672 * g + 96 * PAIRS.index(SAME.get((a, b), (a, b)))
                    pieces.append(value[:, at : at + 96])
                blocks[6 * (place ^ plane) + 3 * g + a] = jnp.concatenate(pieces, axis=1)
    for q in range(4):
        group_ref[4 * q : 4 * q + 4] = (sums[320 * q : 320 * q + 288, :].T * grad_scale).reshape(4, 32, 288)
        for g in range(4):
            out_ref[4 * q + g] = sums[320 * q + 288 : 320 * q + 320, 32 * g : 32 * g + 32] * mean_scale
    owner = lax.axis_index("owner")
    for s in range(owned_ref.shape[1]):
        block = slot_ref[owner, s]
        value = blocks[jnp.maximum(block, 0)]
        owned_ref[:, s, :] = jnp.where(block >= 0, value, 0.0)


def per_device(n_owner, n_dp, activations, out_grad, group_weight, proj_weight, bn_gain, bn_shift, slot_block):
    def swap(value, owner_mask, dp_mask):
        pairs = [
            (o * n_dp + d, (o ^ owner_mask) * n_dp + (d ^ dp_mask)) for o in range(n_owner) for d in range(n_dp)
        ]
        return lax.ppermute(value, AXES, pairs)

    def add_over(value, owner_bits, dp_bits):
        for bit in owner_bits:
            value = value + swap(value, 1 << bit, 0)
        for bit in dp_bits:
            value = value + swap(value, 0, 1 << bit)
        return value

    far_owner = range(2, n_owner.bit_length() - 1)
    far_dp = range(3, n_dp.bit_length() - 1)
    steps = n_dp // 2
    images = activations.shape[0]
    rows = images * 64
    total_rows = rows * n_owner * n_dp
    grad_scale = 1.0 / math.sqrt(total_rows)
    mean_scale = 1.0 / total_rows

    keep, give = call(
        send_kernel,
        [((4, 64, 128), F32)] * 2,
        [pltpu.VMEM(activations.shape, BF16), pltpu.VMEM((8, 64, 128), F32), pltpu.SemaphoreType.DMA],
        activations,
        in_hbm=True,
    )
    taken = swap(give, 1, 0)
    got = [keep, taken]
    for p in range(1, 4):
        got.append(swap(jnp.stack([keep[p], taken[p]]), p & 2, p & 1))

    inputs = [
        activations,
        out_grad,
        group_weight.transpose(0, 2, 1),
        proj_weight,
        bn_gain.reshape(1, -1),
        bn_shift.reshape(1, -1),
    ]
    mine, other = call(
        local_kernel,
        [((16, 104, 128), F32)] * 2,
        [pltpu.VMEM(a.shape, a.dtype) for a in inputs]
        + [
            pltpu.SemaphoreType.DMA((len(inputs),)),
            pltpu.VMEM((4, 1152, 128), BF16),
            pltpu.VMEM((32, 16, rows), BF16),
            pltpu.VMEM((1280, 128), F32),
        ],
        *inputs,
        in_hbm=True,
    )
    total = mine + swap(other, 1, 0)
    total = total[0:4] + swap(total[4:8], 0, 1) + swap(total[8:12], 2, 0) + swap(total[12:16], 2, 1)
    total = total[0] + swap(total[1], 0, 2) + swap(total[2], 0, 4) + swap(total[3], 0, 6)
    total = add_over(total, far_owner, far_dp)

    half = 96 // n_dp
    padded = -(-11 * half // 8) * 8
    pieces = call(
        functools.partial(factor_kernel, steps),
        [((2, padded, 128), F32)] * steps,
        [pltpu.VMEM((2, 288, 1024), BF16), pltpu.VMEM((2 * steps, padded, 128), F32)],
        *got,
    )
    piece = pieces[0]
    for t in range(1, steps):
        piece = piece + swap(pieces[t], 0, 2 * t)
    piece = add_over(piece, far_owner, ())

    total = jnp.concatenate([total] + [swap(total, 0, 2 * z) for z in range(1, 4)])
    own, peer = (jnp.concatenate([total, piece[i]]) for i in range(2))
    near = [own, swap(peer, 0, 1), swap(own, 2, 0), swap(peer, 2, 1)]
    parts = near + [swap(v, 1, 0) for v in near]
    group_grad, proj_grad, out_factor, factor_owned = call(
        functools.partial(finish_kernel, grad_scale, mean_scale),
        [((16, 32, 288), F32), ((512, 512), F32), ((16, 32, 32), F32), ((half, slot_block.shape[1], 288), F32)],
        [pltpu.VMEM((1280, 128), F32), pltpu.VMEM((48, half, 288), F32)],
        slot_block,
        *parts,
    )
    return group_grad.transpose(0, 2, 1), proj_grad, out_factor, factor_owned.transpose(1, 0, 2)


def solution(mesh):
    placed = (P(AXES, None, None, None), P(AXES, None, None, None), P(), P(), P(), P(), P())
    return jax.shard_map(
        functools.partial(per_device, mesh.shape["owner"], mesh.shape["dp"]),
        mesh=mesh,
        in_specs=placed,
        out_specs=(P(), P(), P(), P("owner", "dp", None)),
        check_vma=False,
    )
```

```python
import functools
import math

import jax
import jax.numpy as jnp
from jax import lax
from jax.experimental import pallas as pl
from jax.experimental.pallas import tpu as pltpu
from jax.sharding import PartitionSpec as P

AXES = ("owner", "dp")
F32 = jnp.float32
BF16 = jnp.bfloat16
LOCAL_FLOPS = 4000000000
VMEM_LIMIT = 48 * 1024 * 1024
PAIRS = ((0, 0), (0, 1), (0, 2), (1, 0), (1, 1), (2, 0), (2, 2))
SAME = {(1, 2): (0, 1), (2, 1): (1, 0)}


def whole_vmem():
    return pl.BlockSpec(memory_space=pltpu.VMEM)


def call(body, outs, scratch, *args, in_hbm=False, flops=0):
    def place(arg):
        if arg.dtype == jnp.int32:
            return pl.BlockSpec(memory_space=pltpu.SMEM)
        return pl.BlockSpec(memory_space=pltpu.HBM) if in_hbm else whole_vmem()

    return pl.pallas_call(
        body,
        out_shape=[jax.ShapeDtypeStruct(shape, kind) for shape, kind in outs],
        in_specs=[place(a) for a in args],
        out_specs=[whole_vmem() for _ in outs],
        scratch_shapes=scratch,
        compiler_params=pltpu.CompilerParams(vmem_limit_bytes=VMEM_LIMIT),
        cost_estimate=pl.CostEstimate(flops=flops, bytes_accessed=0, transcendentals=0) if flops else None,
    )(*args)


def plane_id():
    owner, dp = lax.axis_index("owner"), lax.axis_index("dp")
    return (owner & 1) * 4 + ((owner >> 1) & 1) * 2 + (dp & 1)


def cell_id():
    return plane_id() * 4 + ((lax.axis_index("dp") >> 1) & 3)


def send_kernel(x_hbm, *refs):
    out_refs, (x_ref, held, sem) = refs[:4], refs[4:]
    copy = pltpu.make_async_copy(x_hbm, x_ref, sem)
    copy.start()
    me = cell_id()
    copy.wait()
    x_t = x_ref[...].astype(F32).reshape(128, 512).T
    for group in range(16):
        held[group ^ (me & 15)] = x_t[32 * group : 32 * group + 32]
    for place, out in enumerate(out_refs):
        out[...] = held[4 * place : 4 * place + 4]


def shift_rows(value, row_step, col_step):
    images, side, _, width = value.shape
    if col_step != 0:
        flat = value.reshape(images * side, side, width)
        flat = pltpu.roll(flat, (-col_step) % side, 1)
        column = lax.broadcasted_iota(jnp.int32, flat.shape, 1) + col_step
        value = jnp.where((column >= 0) & (column < side), flat, 0.0).reshape(value.shape)
    if row_step != 0:
        edge = jnp.zeros((images, 1, side, width), F32)
        if row_step < 0:
            value = jnp.concatenate([edge, value[:, :-1]], axis=1)
        else:
            value = jnp.concatenate([value[:, 1:], edge], axis=1)
    return value


def diagonal(square):
    lane = lax.broadcasted_iota(jnp.int32, (32, 128), 1)
    out = square[96:128]
    for g in (2, 1, 0):
        out = jnp.where(lane < 32 * (g + 1), square[32 * g : 32 * g + 32], out)
    return out


def local_kernel(*refs):
    sources, (mine_ref, other_ref), held, sems = refs[:6], refs[6:8], refs[8:14], refs[14]
    block_w, hid_t, sums = refs[15:]
    copies = [pltpu.make_async_copy(src, dst, sems.at[i]) for i, (src, dst) in enumerate(zip(sources, held))]
    for copy in copies:
        copy.start()
    x_ref, og_ref, gw_ref, pw_ref, gain_ref, shift_ref = held
    me = cell_id()
    images = x_ref.shape[0]
    rows = images * 64
    for copy in copies:
        copy.wait()
    group_at = lax.broadcasted_iota(jnp.int32, (32, 128), 1) // 32
    for q in range(4):
        stacked = gw_ref[4 * q : 4 * q + 4].astype(F32).reshape(128, 288).T
        for s in range(9):
            for g in range(4):
                at = s * 128 + 32 * g
                block_w[q, at : at + 32, :] = jnp.where(group_at == g, stacked[32 * s : 32 * s + 32], 0.0).astype(BF16)
    x = x_ref[...].astype(F32)
    moved = [
        shift_rows(x, a - 1, b - 1).reshape(rows, 512).astype(BF16) for a in range(3) for b in range(3)
    ]
    conv = []
    for q in range(4):
        lhs = jnp.concatenate([m[:, 128 * q : 128 * q + 128] for m in moved], axis=1)
        conv.append(jnp.dot(lhs, block_w[q], preferred_element_type=F32))
    conv = jnp.concatenate(conv, axis=1)
    gain = gain_ref[...]
    preact = conv * gain + shift_ref[...]
    hidden = jnp.maximum(preact, 0.0)
    og = og_ref[...].reshape(rows, 512)
    back = lax.dot_general(og, pw_ref[...], (((1,), (1,)), ((), ())), preferred_element_type=F32)
    grad = jnp.where(preact > 0.0, back * gain, 0.0).astype(BF16).astype(F32)
    h_t = hidden.T.astype(BF16)
    for j in range(32):
        hid_t[j ^ me] = h_t[16 * j : 16 * j + 16]
    for half, out in enumerate((mine_ref, other_ref)):
        lhs = hid_t[16 * half : 16 * half + 16].reshape(256, rows)
        part = jnp.dot(lhs, og, preferred_element_type=F32)
        for k in range(16):
            for w in range(4):
                out[k, 16 * w : 16 * w + 16, :] = part[16 * k : 16 * k + 16, 128 * w : 128 * w + 128]
    x_t = x.reshape(rows, 512).T.astype(BF16)
    g_t = grad.reshape(rows, 512).T.astype(BF16)
    grad4 = grad.reshape(images, 8, 8, 512)
    back_moved = [
        shift_rows(grad4, 1 - a, 1 - b).reshape(rows, 512).astype(BF16) for a in range(3) for b in range(3)
    ]
    for q in range(4):
        cut = slice(128 * q, 128 * q + 128)
        rhs = jnp.concatenate([m[:, cut] for m in back_moved], axis=1)
        part = jnp.dot(x_t[cut], rhs, preferred_element_type=F32)
        for s in range(9):
            at = 320 * q + 32 * s
            sums[at : at + 32, :] = diagonal(part[:, 128 * s : 128 * s + 128])
        part = jnp.dot(g_t[cut], back_moved[4][:, cut], preferred_element_type=F32)
        sums[320 * q + 288 : 320 * q + 320, :] = diagonal(part)
    for half, out in enumerate((mine_ref, other_ref)):
        for k in range(16):
            j = (16 * half + k) ^ me
            out[k, 64:104, :] = sums[pl.ds(pl.multiple_of(40 * j, 8), 40), :]


def packed_rows(count):
    return 5 * count + -(-count // 4)


def factor_kernel(n_dp, *refs):
    parts, (keep_ref, give_ref), (patches, held) = refs[:7], refs[7:9], refs[9:]
    dp, core = lax.axis_index("dp"), lax.axis_index("owner") & 1
    lane = lax.broadcasted_iota(jnp.int32, (32, 128), 1)
    row, col = (lane >> 3) & 7, lane & 7
    sources = [ref[0] for ref in parts[:4]] + [ref[i] for ref in parts[4:] for i in range(4)]
    for src, x_t in enumerate(sources):
        for a in range(3):
            for b in range(3):
                step = (a - 1) * 8 + b - 1
                value = x_t if step == 0 else pltpu.roll(x_t, (-step) % 128, 1)
                keep = (row + a >= 1) & (row + a <= 8) & (col + b >= 1) & (col + b <= 8)
                at = (3 * a + b) * 32
                patches[at : at + 32, 128 * src : 128 * src + 128] = jnp.where(keep, value, 0.0).astype(BF16)
    pieces = []
    for a, width in ((0, 288), (1, 192), (2, 288)):
        part = lax.dot_general(
            patches[96 * a : 96 * a + 96, :],
            patches[:width, :],
            (((1,), (1,)), ((), ())),
            preferred_element_type=F32,
        )
        for pair in PAIRS:
            if pair[0] == a:
                pieces.append(part[:, 96 * pair[1] : 96 * pair[1] + 96])
    full = jnp.concatenate(pieces, axis=1)
    count = 96 // n_dp // 2
    held[...] = jnp.zeros(held.shape, F32)
    for block in range(2 * n_dp):
        at = (block & 1) ^ core, (block >> 1) ^ dp
        rows = full[count * block : count * block + count]
        for tile in range(5):
            held[at[0], at[1], count * tile : count * tile + count, :] = rows[:, 128 * tile : 128 * tile + 128]
        for i in range(count):
            spot = 5 * count + i // 4
            held[at[0], at[1], spot : spot + 1, 32 * (i % 4) : 32 * (i % 4) + 32] = rows[i : i + 1, 640:672]
    keep_ref[...] = held[0]
    give_ref[...] = held[1]


def finish_kernel(grad_scale, mean_scale, slot_ref, *refs):
    parts, (group_ref, proj_ref, out_ref, owned_ref), (sums, blocks) = refs[:8], refs[8:12], refs[12:]
    me = cell_id()
    count = owned_ref.shape[0] // 2
    step = 104 + packed_rows(count)
    for place, ref in enumerate(parts):
        for z in range(4):
            j = (4 * place + z) ^ me
            base = step * z
            for w in range(4):
                at = pl.multiple_of(16 * j, 16)
                row = base + 16 * w
                proj_ref[pl.ds(at, 16), 128 * w : 128 * w + 128] = ref[row : row + 16, :] * grad_scale
            sums[pl.ds(pl.multiple_of(40 * j, 8), 40), :] = ref[base + 64 : base + 104, :]
            base += 104
            tiles = [ref[base + count * t : base + count * t + count, :] for t in range(5)]
            last = []
            for i in range(count):
                spot = base + 5 * count + i // 4
                last.append(ref[spot : spot + 1, 32 * (i % 4) : 32 * (i % 4) + 32])
            value = jnp.concatenate(tiles + [jnp.concatenate(last, axis=0)], axis=1) * mean_scale
            for a in range(3):
                pieces = []
                for b in range(3):
                    at = 96 * PAIRS.index(SAME.get((a, b), (a, b)))
                    pieces.append(value[:, at : at + 96])
                blocks[j >> 4, 3 * (j & 15) + a] = jnp.concatenate(pieces, axis=1)
    for q in range(4):
        group_ref[4 * q : 4 * q + 4] = (sums[320 * q : 320 * q + 288, :].T * grad_scale).reshape(4, 32, 288)
        for g in range(4):
            out_ref[4 * q + g] = sums[320 * q + 288 : 320 * q + 320, 32 * g : 32 * g + 32] * mean_scale
    owner = lax.axis_index("owner")
    for s in range(owned_ref.shape[1]):
        block = slot_ref[owner, s]
        for core in range(2):
            value = blocks[core, jnp.maximum(block, 0)]
            owned_ref[count * core : count * core + count, s, :] = jnp.where(block >= 0, value, 0.0)


def per_device(n_owner, n_dp, activations, out_grad, group_weight, proj_weight, bn_gain, bn_shift, slot_block):
    def swap(value, owner_mask, dp_mask):
        pairs = [
            (o * n_dp + d, (o ^ owner_mask) * n_dp + (d ^ dp_mask)) for o in range(n_owner) for d in range(n_dp)
        ]
        return lax.ppermute(value, AXES, pairs)

    def add_over(value, owner_bits, dp_bits):
        for bit in owner_bits:
            value = value + swap(value, 1 << bit, 0)
        for bit in dp_bits:
            value = value + swap(value, 0, 1 << bit)
        return value

    far_owner = range(2, n_owner.bit_length() - 1)
    far_dp = range(3, n_dp.bit_length() - 1)
    images = activations.shape[0]
    rows = images * 64
    total_rows = rows * n_owner * n_dp
    grad_scale = 1.0 / math.sqrt(total_rows)
    mean_scale = 1.0 / total_rows

    sent = call(
        send_kernel,
        [((4, 32, 128), F32)] * 4,
        [pltpu.VMEM(activations.shape, BF16), pltpu.VMEM((16, 32, 128), F32), pltpu.SemaphoreType.DMA],
        activations,
        in_hbm=True,
    )
    got = [sent[0], swap(sent[1], 0, 1), swap(sent[2], 2, 0), swap(sent[3], 2, 1)]

    inputs = [
        activations,
        out_grad,
        group_weight.transpose(0, 2, 1),
        proj_weight,
        bn_gain.reshape(1, -1),
        bn_shift.reshape(1, -1),
    ]
    mine, other = call(
        local_kernel,
        [((16, 104, 128), F32)] * 2,
        [pltpu.VMEM(a.shape, a.dtype) for a in inputs]
        + [
            pltpu.SemaphoreType.DMA((len(inputs),)),
            pltpu.VMEM((4, 1152, 128), BF16),
            pltpu.VMEM((32, 16, rows), BF16),
            pltpu.VMEM((1280, 128), F32),
        ],
        *inputs,
        in_hbm=True,
        flops=LOCAL_FLOPS,
    )
    total = mine + swap(other, 1, 0)
    far = [swap(jnp.stack([v[z] for v in got]), 0, 2 * z) for z in range(1, 4)]
    total = total[0:4] + swap(total[4:8], 0, 1) + swap(total[8:12], 2, 0) + swap(total[12:16], 2, 1)
    total = total[0] + swap(total[1], 0, 2) + swap(total[2], 0, 4) + swap(total[3], 0, 6)
    total = add_over(total, far_owner, far_dp)

    half = 96 // n_dp
    packed = packed_rows(half // 2)
    keep, give = call(
        functools.partial(factor_kernel, n_dp),
        [((n_dp, packed, 128), F32)] * 2,
        [pltpu.VMEM((288, 2048), BF16), pltpu.VMEM((2, n_dp, packed, 128), F32)],
        *got,
        *far,
    )
    piece = add_over(keep + swap(give, 1, 0), far_owner, ())
    for bit in reversed(far_dp):
        near = piece.shape[0] // 2
        piece = piece[:near] + swap(piece[near:], 0, 1 << bit)
    piece = piece.reshape(4, 2 * packed, 128)

    line = [jnp.concatenate([total, piece[z]]) for z in range(4)]
    line = [line[0]] + [swap(line[z], 0, 2 * z) for z in range(1, 4)]
    own = jnp.concatenate([v[: 104 + packed] for v in line])
    peer = jnp.concatenate([w for v in line for w in (v[:104], v[104 + packed :])])
    near = [own, swap(peer, 0, 1), swap(own, 2, 0), swap(peer, 2, 1)]
    parts = near + [swap(v, 1, 0) for v in near]
    slots = slot_block.shape[1]
    group_grad, proj_grad, out_factor, factor_owned = call(
        functools.partial(finish_kernel, grad_scale, mean_scale),
        [((16, 32, 288), F32), ((512, 512), F32), ((16, 32, 32), F32), ((half, slots, 288), F32)],
        [pltpu.VMEM((1280, 128), F32), pltpu.VMEM((2, 48, half // 2, 288), F32)],
        slot_block,
        *parts,
    )
    return group_grad.transpose(0, 2, 1), proj_grad, out_factor, factor_owned.transpose(1, 0, 2)


def solution(mesh):
    placed = (P(AXES, None, None, None), P(AXES, None, None, None), P(), P(), P(), P(), P())
    return jax.shard_map(
        functools.partial(per_device, mesh.shape["owner"], mesh.shape["dp"]),
        mesh=mesh,
        in_specs=placed,
        out_specs=(P(), P(), P(), P("owner", "dp", None)),
        check_vma=False,
    )
```

```python
import functools
import math

import jax
import jax.numpy as jnp
from jax import lax
from jax.experimental import pallas as pl
from jax.experimental.pallas import tpu as pltpu
from jax.sharding import PartitionSpec as P

AXES = ("owner", "dp")
F32 = jnp.float32
BF16 = jnp.bfloat16
SEND_FLOPS = 6000000000
LOCAL_FLOPS = 4000000000
VMEM_LIMIT = 48 * 1024 * 1024
PAIRS = ((0, 0), (0, 1), (0, 2), (1, 0), (1, 1), (2, 0), (2, 2))
SAME = {(1, 2): (0, 1), (2, 1): (1, 0)}


def whole_vmem():
    return pl.BlockSpec(memory_space=pltpu.VMEM)


def call(body, outs, scratch, *args, in_hbm=False, flops=0):
    def place(arg):
        if arg.dtype == jnp.int32:
            return pl.BlockSpec(memory_space=pltpu.SMEM)
        return pl.BlockSpec(memory_space=pltpu.HBM) if in_hbm else whole_vmem()

    return pl.pallas_call(
        body,
        out_shape=[jax.ShapeDtypeStruct(shape, kind) for shape, kind in outs],
        in_specs=[place(a) for a in args],
        out_specs=[whole_vmem() for _ in outs],
        scratch_shapes=scratch,
        compiler_params=pltpu.CompilerParams(vmem_limit_bytes=VMEM_LIMIT),
        cost_estimate=pl.CostEstimate(flops=flops, bytes_accessed=0, transcendentals=0) if flops else None,
    )(*args)


def plane_id():
    owner, dp = lax.axis_index("owner"), lax.axis_index("dp")
    return (owner & 1) * 4 + ((owner >> 1) & 1) * 2 + (dp & 1)


def cell_id():
    return plane_id() * 4 + ((lax.axis_index("dp") >> 1) & 3)


def send_kernel(x_hbm, *refs):
    out_refs, (x_ref, held, sem) = refs[:4], refs[4:]
    copy = pltpu.make_async_copy(x_hbm, x_ref, sem)
    copy.start()
    me = cell_id()
    copy.wait()
    x_t = x_ref[...].astype(F32).reshape(128, 512).T
    for group in range(16):
        held[group ^ (me & 15)] = x_t[32 * group : 32 * group + 32]
    for place, out in enumerate(out_refs):
        out[...] = held[4 * place : 4 * place + 4]


def shift_rows(value, row_step, col_step):
    images, side, _, width = value.shape
    if col_step != 0:
        flat = value.reshape(images * side, side, width)
        flat = pltpu.roll(flat, (-col_step) % side, 1)
        column = lax.broadcasted_iota(jnp.int32, flat.shape, 1) + col_step
        value = jnp.where((column >= 0) & (column < side), flat, 0.0).reshape(value.shape)
    if row_step != 0:
        edge = jnp.zeros((images, 1, side, width), F32)
        if row_step < 0:
            value = jnp.concatenate([edge, value[:, :-1]], axis=1)
        else:
            value = jnp.concatenate([value[:, 1:], edge], axis=1)
    return value


def diagonal(square):
    lane = lax.broadcasted_iota(jnp.int32, (32, 128), 1)
    out = square[96:128]
    for g in (2, 1, 0):
        out = jnp.where(lane < 32 * (g + 1), square[32 * g : 32 * g + 32], out)
    return out


def local_kernel(*refs):
    sources, (mine_ref, other_ref), held, sems = refs[:6], refs[6:8], refs[8:14], refs[14]
    block_w, hid_t, sums = refs[15:]
    copies = [pltpu.make_async_copy(src, dst, sems.at[i]) for i, (src, dst) in enumerate(zip(sources, held))]
    for copy in copies:
        copy.start()
    x_ref, og_ref, gw_ref, pw_ref, gain_ref, shift_ref = held
    me = cell_id()
    images = x_ref.shape[0]
    rows = images * 64
    for copy in copies:
        copy.wait()
    group_at = lax.broadcasted_iota(jnp.int32, (32, 128), 1) // 32
    for q in range(4):
        stacked = gw_ref[4 * q : 4 * q + 4].astype(F32).reshape(128, 288).T
        for s in range(9):
            for g in range(4):
                at = s * 128 + 32 * g
                block_w[q, at : at + 32, :] = jnp.where(group_at == g, stacked[32 * s : 32 * s + 32], 0.0).astype(BF16)
    x = x_ref[...].astype(F32)
    moved = [
        shift_rows(x, a - 1, b - 1).reshape(rows, 512).astype(BF16) for a in range(3) for b in range(3)
    ]
    conv = []
    for q in range(4):
        lhs = jnp.concatenate([m[:, 128 * q : 128 * q + 128] for m in moved], axis=1)
        conv.append(jnp.dot(lhs, block_w[q], preferred_element_type=F32))
    conv = jnp.concatenate(conv, axis=1)
    gain = gain_ref[...]
    preact = conv * gain + shift_ref[...]
    hidden = jnp.maximum(preact, 0.0)
    og = og_ref[...].reshape(rows, 512)
    back = lax.dot_general(og, pw_ref[...], (((1,), (1,)), ((), ())), preferred_element_type=F32)
    grad = jnp.where(preact > 0.0, back * gain, 0.0).astype(BF16).astype(F32)
    h_t = hidden.T.astype(BF16)
    for j in range(32):
        hid_t[j ^ me] = h_t[16 * j : 16 * j + 16]
    for half, out in enumerate((mine_ref, other_ref)):
        lhs = hid_t[16 * half : 16 * half + 16].reshape(256, rows)
        part = jnp.dot(lhs, og, preferred_element_type=F32)
        for k in range(16):
            for w in range(4):
                out[k, 16 * w : 16 * w + 16, :] = part[16 * k : 16 * k + 16, 128 * w : 128 * w + 128]
    x_t = x.reshape(rows, 512).T.astype(BF16)
    g_t = grad.reshape(rows, 512).T.astype(BF16)
    grad4 = grad.reshape(images, 8, 8, 512)
    back_moved = [
        shift_rows(grad4, 1 - a, 1 - b).reshape(rows, 512).astype(BF16) for a in range(3) for b in range(3)
    ]
    for q in range(4):
        cut = slice(128 * q, 128 * q + 128)
        rhs = jnp.concatenate([m[:, cut] for m in back_moved], axis=1)
        part = jnp.dot(x_t[cut], rhs, preferred_element_type=F32)
        for s in range(9):
            at = 320 * q + 32 * s
            sums[at : at + 32, :] = diagonal(part[:, 128 * s : 128 * s + 128])
        part = jnp.dot(g_t[cut], back_moved[4][:, cut], preferred_element_type=F32)
        sums[320 * q + 288 : 320 * q + 320, :] = diagonal(part)
    for half, out in enumerate((mine_ref, other_ref)):
        for k in range(16):
            j = (16 * half + k) ^ me
            out[k, 64:104, :] = sums[pl.ds(pl.multiple_of(40 * j, 8), 40), :]


def packed_rows(count):
    return 5 * count + -(-count // 4)


def factor_kernel(n_dp, *refs):
    parts, (keep_ref, give_ref), (patches, held) = refs[:7], refs[7:9], refs[9:]
    dp, core = lax.axis_index("dp"), lax.axis_index("owner") & 1
    lane = lax.broadcasted_iota(jnp.int32, (32, 128), 1)
    row, col = (lane >> 3) & 7, lane & 7
    sources = [ref[0] for ref in parts[:4]] + [ref[i] for ref in parts[4:] for i in range(4)]
    for src, x_t in enumerate(sources):
        for a in range(3):
            for b in range(3):
                step = (a - 1) * 8 + b - 1
                value = x_t if step == 0 else pltpu.roll(x_t, (-step) % 128, 1)
                keep = (row + a >= 1) & (row + a <= 8) & (col + b >= 1) & (col + b <= 8)
                at = (3 * a + b) * 32
                patches[at : at + 32, 128 * src : 128 * src + 128] = jnp.where(keep, value, 0.0).astype(BF16)
    pieces = []
    for a, width in ((0, 288), (1, 192), (2, 288)):
        part = lax.dot_general(
            patches[96 * a : 96 * a + 96, :],
            patches[:width, :],
            (((1,), (1,)), ((), ())),
            preferred_element_type=F32,
        )
        for pair in PAIRS:
            if pair[0] == a:
                pieces.append(part[:, 96 * pair[1] : 96 * pair[1] + 96])
    full = jnp.concatenate(pieces, axis=1)
    count = 96 // n_dp // 2
    held[...] = jnp.zeros(held.shape, F32)
    for block in range(2 * n_dp):
        at = (block & 1) ^ core, (block >> 1) ^ dp
        rows = full[count * block : count * block + count]
        for tile in range(5):
            held[at[0], at[1], count * tile : count * tile + count, :] = rows[:, 128 * tile : 128 * tile + 128]
        for i in range(count):
            spot = 5 * count + i // 4
            held[at[0], at[1], spot : spot + 1, 32 * (i % 4) : 32 * (i % 4) + 32] = rows[i : i + 1, 640:672]
    keep_ref[...] = held[0]
    give_ref[...] = held[1]


def line_kernel(total_ref, piece_ref, first_ref, first_peer_ref, *line_refs):
    total = total_ref[...]
    size = first_ref.shape[0]
    first_ref[:104, :] = total
    first_ref[104:, :] = piece_ref[0, : size - 104, :]
    first_peer_ref[:104, :] = total
    first_peer_ref[104:, :] = piece_ref[0, size - 104 :, :]
    for z, ref in enumerate(line_refs):
        ref[:104, :] = total
        ref[104:, :] = piece_ref[z + 1]


def merge_kernel(*refs):
    parts, (own_ref, peer_ref) = refs[:3], refs[3:]
    size = own_ref.shape[0] // 3
    for z, ref in enumerate(parts):
        at = size * z
        own_ref[at : at + size, :] = ref[:size, :]
        peer_ref[at : at + 104, :] = ref[:104, :]
        peer_ref[at + 104 : at + size, :] = ref[size:, :]


def finish_kernel(grad_scale, mean_scale, slot_ref, *refs):
    parts, (group_ref, proj_ref, out_ref, owned_ref), (sums, blocks) = refs[:13], refs[13:17], refs[17:]
    me = cell_id()
    count = owned_ref.shape[0] // 2
    step = 104 + packed_rows(count)
    for place in range(8):
        for z in range(4):
            j = (4 * place + z) ^ me
            if z > 0:
                ref, base = parts[5 + place], step * (z - 1)
            elif place < 4:
                ref, base = parts[place], 0
            else:
                ref, base = parts[4].at[place - 4], 0
            for w in range(4):
                at = pl.multiple_of(16 * j, 16)
                row = base + 16 * w
                proj_ref[pl.ds(at, 16), 128 * w : 128 * w + 128] = ref[row : row + 16, :] * grad_scale
            sums[pl.ds(pl.multiple_of(40 * j, 8), 40), :] = ref[base + 64 : base + 104, :]
            base += 104
            tiles = [ref[base + count * t : base + count * t + count, :] for t in range(5)]
            last = []
            for i in range(count):
                spot = base + 5 * count + i // 4
                last.append(ref[spot : spot + 1, 32 * (i % 4) : 32 * (i % 4) + 32])
            value = jnp.concatenate(tiles + [jnp.concatenate(last, axis=0)], axis=1) * mean_scale
            for a in range(3):
                pieces = []
                for b in range(3):
                    at = 96 * PAIRS.index(SAME.get((a, b), (a, b)))
                    pieces.append(value[:, at : at + 96])
                blocks[j >> 4, 3 * (j & 15) + a] = jnp.concatenate(pieces, axis=1)
    for q in range(4):
        group_ref[4 * q : 4 * q + 4] = (sums[320 * q : 320 * q + 288, :].T * grad_scale).reshape(4, 32, 288)
        for g in range(4):
            out_ref[4 * q + g] = sums[320 * q + 288 : 320 * q + 320, 32 * g : 32 * g + 32] * mean_scale
    owner = lax.axis_index("owner")
    for s in range(owned_ref.shape[1]):
        block = slot_ref[owner, s]
        for core in range(2):
            value = blocks[core, jnp.maximum(block, 0)]
            owned_ref[count * core : count * core + count, s, :] = jnp.where(block >= 0, value, 0.0)


def per_device(n_owner, n_dp, activations, out_grad, group_weight, proj_weight, bn_gain, bn_shift, slot_block):
    def swap(value, owner_mask, dp_mask):
        pairs = [
            (o * n_dp + d, (o ^ owner_mask) * n_dp + (d ^ dp_mask)) for o in range(n_owner) for d in range(n_dp)
        ]
        return lax.ppermute(value, AXES, pairs)

    def add_over(value, owner_bits, dp_bits):
        for bit in owner_bits:
            value = value + swap(value, 1 << bit, 0)
        for bit in dp_bits:
            value = value + swap(value, 0, 1 << bit)
        return value

    far_owner = range(2, n_owner.bit_length() - 1)
    far_dp = range(3, n_dp.bit_length() - 1)
    images = activations.shape[0]
    rows = images * 64
    total_rows = rows * n_owner * n_dp
    grad_scale = 1.0 / math.sqrt(total_rows)
    mean_scale = 1.0 / total_rows

    sent = call(
        send_kernel,
        [((4, 32, 128), F32)] * 4,
        [pltpu.VMEM(activations.shape, BF16), pltpu.VMEM((16, 32, 128), F32), pltpu.SemaphoreType.DMA],
        activations,
        in_hbm=True,
        flops=SEND_FLOPS,
    )
    inputs = [
        activations,
        out_grad,
        group_weight.transpose(0, 2, 1),
        proj_weight,
        bn_gain.reshape(1, -1),
        bn_shift.reshape(1, -1),
    ]
    mine, other = call(
        local_kernel,
        [((16, 104, 128), F32)] * 2,
        [pltpu.VMEM(a.shape, a.dtype) for a in inputs]
        + [
            pltpu.SemaphoreType.DMA((len(inputs),)),
            pltpu.VMEM((4, 1152, 128), BF16),
            pltpu.VMEM((32, 16, rows), BF16),
            pltpu.VMEM((1280, 128), F32),
        ],
        *inputs,
        in_hbm=True,
        flops=LOCAL_FLOPS,
    )
    sent, other = lax.optimization_barrier((sent, other))
    got = [sent[0], swap(sent[1], 0, 1), swap(sent[2], 2, 0), swap(sent[3], 2, 1)]
    total = mine + swap(other, 1, 0)
    total, got = lax.optimization_barrier((total, got))
    far = [swap(jnp.stack([v[z] for v in got]), 0, 2 * z) for z in range(1, 4)]
    total = total[0:4] + swap(total[4:8], 0, 1) + swap(total[8:12], 2, 0) + swap(total[12:16], 2, 1)
    half = 96 // n_dp
    packed = packed_rows(half // 2)
    keep, give = call(
        functools.partial(factor_kernel, n_dp),
        [((n_dp, packed, 128), F32)] * 2,
        [pltpu.VMEM((288, 2048), BF16), pltpu.VMEM((2, n_dp, packed, 128), F32)],
        *got,
        *far,
    )
    give, total = lax.optimization_barrier((give, total))
    total = total[0] + swap(total[1], 0, 2) + swap(total[2], 0, 4) + swap(total[3], 0, 6)
    total = add_over(total, far_owner, far_dp)

    piece = add_over(keep + swap(give, 1, 0), far_owner, ())
    for bit in reversed(far_dp):
        near = piece.shape[0] // 2
        piece = piece[:near] + swap(piece[near:], 0, 1 << bit)
    piece = piece.reshape(4, 2 * packed, 128)

    first, first_peer, *line = call(
        line_kernel,
        [((104 + packed, 128), F32)] * 2 + [((104 + 2 * packed, 128), F32)] * 3,
        [],
        total,
        piece,
    )
    line = [swap(line[z - 1], 0, 2 * z) for z in range(1, 4)]
    early = [first, swap(first_peer, 0, 1), swap(first, 2, 0), swap(first_peer, 2, 1)]
    own, peer = call(merge_kernel, [((3 * (104 + packed), 128), F32)] * 2, [], *line)
    late = [own, swap(peer, 0, 1), swap(own, 2, 0), swap(peer, 2, 1)]
    parts = early + [swap(jnp.stack(early), 1, 0)] + late + [swap(v, 1, 0) for v in late]
    slots = slot_block.shape[1]
    group_grad, proj_grad, out_factor, factor_owned = call(
        functools.partial(finish_kernel, grad_scale, mean_scale),
        [((16, 32, 288), F32), ((512, 512), F32), ((16, 32, 32), F32), ((half, slots, 288), F32)],
        [pltpu.VMEM((1280, 128), F32), pltpu.VMEM((2, 48, half // 2, 288), F32)],
        slot_block,
        *parts,
    )
    return group_grad.transpose(0, 2, 1), proj_grad, out_factor, factor_owned.transpose(1, 0, 2)


def solution(mesh):
    placed = (P(AXES, None, None, None), P(AXES, None, None, None), P(), P(), P(), P(), P())
    return jax.shard_map(
        functools.partial(per_device, mesh.shape["owner"], mesh.shape["dp"]),
        mesh=mesh,
        in_specs=placed,
        out_specs=(P(), P(), P(), P("owner", "dp", None)),
        check_vma=False,
    )
```

```python
import functools
import math

import jax
import jax.numpy as jnp
from jax import lax
from jax.experimental import pallas as pl
from jax.experimental.pallas import tpu as pltpu
from jax.sharding import PartitionSpec as P

AXES = ("owner", "dp")
F32 = jnp.float32
BF16 = jnp.bfloat16
STACK_FLOPS = 4000000000
FACTOR_FLOPS = 4000000000
FIRST_FLOPS = 4000000000
AFTER_CORE = AFTER_PLANE = AFTER_LINE = True
SEND_FLOPS = 6000000000
LOCAL_FLOPS = 4000000000
VMEM_LIMIT = 48 * 1024 * 1024
PAIRS = ((0, 0), (0, 1), (0, 2), (1, 0), (1, 1), (2, 0), (2, 2))
SAME = {(1, 2): (0, 1), (2, 1): (1, 0)}


def whole_vmem():
    return pl.BlockSpec(memory_space=pltpu.VMEM)


def call(body, outs, scratch, *args, in_hbm=False, flops=0, after=()):
    count = len(args)

    def run(*refs):
        body(*refs[:count], *refs[count + len(after) :])

    def place(arg):
        if arg.dtype == jnp.int32:
            return pl.BlockSpec(memory_space=pltpu.SMEM)
        return pl.BlockSpec(memory_space=pltpu.HBM) if in_hbm else whole_vmem()

    return pl.pallas_call(
        run,
        out_shape=[jax.ShapeDtypeStruct(shape, kind) for shape, kind in outs],
        in_specs=[place(a) for a in args] + [pl.BlockSpec(memory_space=pl.ANY) for _ in after],
        out_specs=[whole_vmem() for _ in outs],
        scratch_shapes=scratch,
        compiler_params=pltpu.CompilerParams(vmem_limit_bytes=VMEM_LIMIT),
        cost_estimate=pl.CostEstimate(flops=flops, bytes_accessed=0, transcendentals=0) if flops else None,
    )(*args, *after)


def plane_id():
    owner, dp = lax.axis_index("owner"), lax.axis_index("dp")
    return (owner & 1) * 4 + ((owner >> 1) & 1) * 2 + (dp & 1)


def cell_id():
    return plane_id() * 4 + ((lax.axis_index("dp") >> 1) & 3)


def send_kernel(x_hbm, *refs):
    out_refs, (x_ref, held, sem) = refs[:4], refs[4:]
    copy = pltpu.make_async_copy(x_hbm, x_ref, sem)
    copy.start()
    me = cell_id()
    copy.wait()
    x_t = x_ref[...].astype(F32).reshape(128, 512).T
    for group in range(16):
        held[group ^ (me & 15)] = x_t[32 * group : 32 * group + 32]
    for place, out in enumerate(out_refs):
        out[...] = held[4 * place : 4 * place + 4]


def shift_rows(value, row_step, col_step):
    images, side, _, width = value.shape
    if col_step != 0:
        flat = value.reshape(images * side, side, width)
        flat = pltpu.roll(flat, (-col_step) % side, 1)
        column = lax.broadcasted_iota(jnp.int32, flat.shape, 1) + col_step
        value = jnp.where((column >= 0) & (column < side), flat, 0.0).reshape(value.shape)
    if row_step != 0:
        edge = jnp.zeros((images, 1, side, width), F32)
        if row_step < 0:
            value = jnp.concatenate([edge, value[:, :-1]], axis=1)
        else:
            value = jnp.concatenate([value[:, 1:], edge], axis=1)
    return value


def diagonal(square):
    lane = lax.broadcasted_iota(jnp.int32, (32, 128), 1)
    out = square[96:128]
    for g in (2, 1, 0):
        out = jnp.where(lane < 32 * (g + 1), square[32 * g : 32 * g + 32], out)
    return out


def local_kernel(*refs):
    sources, (mine_ref, other_ref), held, sems = refs[:6], refs[6:8], refs[8:14], refs[14]
    block_w, hid_t, sums = refs[15:]
    copies = [pltpu.make_async_copy(src, dst, sems.at[i]) for i, (src, dst) in enumerate(zip(sources, held))]
    for copy in copies:
        copy.start()
    x_ref, og_ref, gw_ref, pw_ref, gain_ref, shift_ref = held
    me = cell_id()
    images = x_ref.shape[0]
    rows = images * 64
    for copy in copies:
        copy.wait()
    group_at = lax.broadcasted_iota(jnp.int32, (32, 128), 1) // 32
    for q in range(4):
        stacked = gw_ref[4 * q : 4 * q + 4].astype(F32).reshape(128, 288).T
        for s in range(9):
            for g in range(4):
                at = s * 128 + 32 * g
                block_w[q, at : at + 32, :] = jnp.where(group_at == g, stacked[32 * s : 32 * s + 32], 0.0).astype(BF16)
    x = x_ref[...].astype(F32)
    moved = [
        shift_rows(x, a - 1, b - 1).reshape(rows, 512).astype(BF16) for a in range(3) for b in range(3)
    ]
    conv = []
    for q in range(4):
        lhs = jnp.concatenate([m[:, 128 * q : 128 * q + 128] for m in moved], axis=1)
        conv.append(jnp.dot(lhs, block_w[q], preferred_element_type=F32))
    conv = jnp.concatenate(conv, axis=1)
    gain = gain_ref[...]
    preact = conv * gain + shift_ref[...]
    hidden = jnp.maximum(preact, 0.0)
    og = og_ref[...].reshape(rows, 512)
    back = lax.dot_general(og, pw_ref[...], (((1,), (1,)), ((), ())), preferred_element_type=F32)
    grad = jnp.where(preact > 0.0, back * gain, 0.0).astype(BF16).astype(F32)
    h_t = hidden.T.astype(BF16)
    for j in range(32):
        hid_t[j ^ me] = h_t[16 * j : 16 * j + 16]
    for half, out in enumerate((mine_ref, other_ref)):
        lhs = hid_t[16 * half : 16 * half + 16].reshape(256, rows)
        part = jnp.dot(lhs, og, preferred_element_type=F32)
        for k in range(16):
            for w in range(4):
                out[k, 16 * w : 16 * w + 16, :] = part[16 * k : 16 * k + 16, 128 * w : 128 * w + 128]
    x_t = x.reshape(rows, 512).T.astype(BF16)
    g_t = grad.reshape(rows, 512).T.astype(BF16)
    grad4 = grad.reshape(images, 8, 8, 512)
    back_moved = [
        shift_rows(grad4, 1 - a, 1 - b).reshape(rows, 512).astype(BF16) for a in range(3) for b in range(3)
    ]
    for q in range(4):
        cut = slice(128 * q, 128 * q + 128)
        rhs = jnp.concatenate([m[:, cut] for m in back_moved], axis=1)
        part = jnp.dot(x_t[cut], rhs, preferred_element_type=F32)
        for s in range(9):
            at = 320 * q + 32 * s
            sums[at : at + 32, :] = diagonal(part[:, 128 * s : 128 * s + 128])
        part = jnp.dot(g_t[cut], back_moved[4][:, cut], preferred_element_type=F32)
        sums[320 * q + 288 : 320 * q + 320, :] = diagonal(part)
    for half, out in enumerate((mine_ref, other_ref)):
        for k in range(16):
            j = (16 * half + k) ^ me
            out[k, 64:104, :] = sums[pl.ds(pl.multiple_of(40 * j, 8), 40), :]


def packed_rows(count):
    return 5 * count + -(-count // 4)


def factor_kernel(n_dp, *refs):
    parts, (keep_ref, give_ref), (patches, held) = refs[:7], refs[7:9], refs[9:]
    dp, core = lax.axis_index("dp"), lax.axis_index("owner") & 1
    lane = lax.broadcasted_iota(jnp.int32, (32, 128), 1)
    row, col = (lane >> 3) & 7, lane & 7
    sources = [ref[0] for ref in parts[:4]] + [ref[i] for ref in parts[4:] for i in range(4)]
    for src, x_t in enumerate(sources):
        for a in range(3):
            for b in range(3):
                step = (a - 1) * 8 + b - 1
                value = x_t if step == 0 else pltpu.roll(x_t, (-step) % 128, 1)
                keep = (row + a >= 1) & (row + a <= 8) & (col + b >= 1) & (col + b <= 8)
                at = (3 * a + b) * 32
                patches[at : at + 32, 128 * src : 128 * src + 128] = jnp.where(keep, value, 0.0).astype(BF16)
    pieces = []
    for a, width in ((0, 288), (1, 192), (2, 288)):
        part = lax.dot_general(
            patches[96 * a : 96 * a + 96, :],
            patches[:width, :],
            (((1,), (1,)), ((), ())),
            preferred_element_type=F32,
        )
        for pair in PAIRS:
            if pair[0] == a:
                pieces.append(part[:, 96 * pair[1] : 96 * pair[1] + 96])
    full = jnp.concatenate(pieces, axis=1)
    count = 96 // n_dp // 2
    held[...] = jnp.zeros(held.shape, F32)
    for block in range(2 * n_dp):
        at = (block & 1) ^ core, (block >> 1) ^ dp
        rows = full[count * block : count * block + count]
        for tile in range(5):
            held[at[0], at[1], count * tile : count * tile + count, :] = rows[:, 128 * tile : 128 * tile + 128]
        for i in range(count):
            spot = 5 * count + i // 4
            held[at[0], at[1], spot : spot + 1, 32 * (i % 4) : 32 * (i % 4) + 32] = rows[i : i + 1, 640:672]
    keep_ref[...] = held[0]
    give_ref[...] = held[1]


def stack_kernel(*refs):
    for z, out in enumerate(refs[4:]):
        for i, ref in enumerate(refs[:4]):
            out[i] = ref[z + 1]


def copy_kernel(src_ref, out_ref):
    out_ref[...] = src_ref[...]


def line_kernel(total_ref, piece_ref, *line_refs):
    for z, ref in enumerate(line_refs):
        ref[:104, :] = total_ref[...]
        ref[104:, :] = piece_ref[z + 1]


def first_kernel(total_ref, piece_ref, first_ref, peer_ref):
    size = first_ref.shape[0]
    for ref, at in ((first_ref, 0), (peer_ref, size - 104)):
        ref[:104, :] = total_ref[...]
        ref[104:, :] = piece_ref[0, at : at + size - 104, :]


def merge_kernel(*refs):
    parts, (own_ref, peer_ref) = refs[:3], refs[3:]
    size = own_ref.shape[0] // 3
    for z, ref in enumerate(parts):
        at = size * z
        own_ref[at : at + size, :] = ref[:size, :]
        peer_ref[at : at + 104, :] = ref[:104, :]
        peer_ref[at + 104 : at + size, :] = ref[size:, :]


def finish_kernel(grad_scale, mean_scale, slot_ref, *refs):
    parts, (group_ref, proj_ref, out_ref, owned_ref), (sums, blocks) = refs[:13], refs[13:17], refs[17:]
    me = cell_id()
    count = owned_ref.shape[0] // 2
    step = 104 + packed_rows(count)
    for place in range(8):
        for z in range(4):
            j = (4 * place + z) ^ me
            if z > 0:
                ref, base = parts[5 + place], step * (z - 1)
            elif place < 4:
                ref, base = parts[place], 0
            else:
                ref, base = parts[4].at[place - 4], 0
            for w in range(4):
                at = pl.multiple_of(16 * j, 16)
                row = base + 16 * w
                proj_ref[pl.ds(at, 16), 128 * w : 128 * w + 128] = ref[row : row + 16, :] * grad_scale
            sums[pl.ds(pl.multiple_of(40 * j, 8), 40), :] = ref[base + 64 : base + 104, :]
            base += 104
            tiles = [ref[base + count * t : base + count * t + count, :] for t in range(5)]
            last = []
            for i in range(count):
                spot = base + 5 * count + i // 4
                last.append(ref[spot : spot + 1, 32 * (i % 4) : 32 * (i % 4) + 32])
            value = jnp.concatenate(tiles + [jnp.concatenate(last, axis=0)], axis=1) * mean_scale
            for a in range(3):
                pieces = []
                for b in range(3):
                    at = 96 * PAIRS.index(SAME.get((a, b), (a, b)))
                    pieces.append(value[:, at : at + 96])
                blocks[j >> 4, 3 * (j & 15) + a] = jnp.concatenate(pieces, axis=1)
    for q in range(4):
        group_ref[4 * q : 4 * q + 4] = (sums[320 * q : 320 * q + 288, :].T * grad_scale).reshape(4, 32, 288)
        for g in range(4):
            out_ref[4 * q + g] = sums[320 * q + 288 : 320 * q + 320, 32 * g : 32 * g + 32] * mean_scale
    owner = lax.axis_index("owner")
    for s in range(owned_ref.shape[1]):
        block = slot_ref[owner, s]
        for core in range(2):
            value = blocks[core, jnp.maximum(block, 0)]
            owned_ref[count * core : count * core + count, s, :] = jnp.where(block >= 0, value, 0.0)


def per_device(n_owner, n_dp, activations, out_grad, group_weight, proj_weight, bn_gain, bn_shift, slot_block):
    def swap(value, owner_mask, dp_mask):
        pairs = [
            (o * n_dp + d, (o ^ owner_mask) * n_dp + (d ^ dp_mask)) for o in range(n_owner) for d in range(n_dp)
        ]
        return lax.ppermute(value, AXES, pairs)

    def add_over(value, owner_bits, dp_bits):
        for bit in owner_bits:
            value = value + swap(value, 1 << bit, 0)
        for bit in dp_bits:
            value = value + swap(value, 0, 1 << bit)
        return value

    far_owner = range(2, n_owner.bit_length() - 1)
    far_dp = range(3, n_dp.bit_length() - 1)
    images = activations.shape[0]
    rows = images * 64
    total_rows = rows * n_owner * n_dp
    grad_scale = 1.0 / math.sqrt(total_rows)
    mean_scale = 1.0 / total_rows

    sent = call(
        send_kernel,
        [((4, 32, 128), F32)] * 4,
        [pltpu.VMEM(activations.shape, BF16), pltpu.VMEM((16, 32, 128), F32), pltpu.SemaphoreType.DMA],
        activations,
        in_hbm=True,
        flops=SEND_FLOPS,
    )
    inputs = [
        activations,
        out_grad,
        group_weight.transpose(0, 2, 1),
        proj_weight,
        bn_gain.reshape(1, -1),
        bn_shift.reshape(1, -1),
    ]
    mine, other = call(
        local_kernel,
        [((16, 104, 128), F32)] * 2,
        [pltpu.VMEM(a.shape, a.dtype) for a in inputs]
        + [
            pltpu.SemaphoreType.DMA((len(inputs),)),
            pltpu.VMEM((4, 1152, 128), BF16),
            pltpu.VMEM((32, 16, rows), BF16),
            pltpu.VMEM((1280, 128), F32),
        ],
        *inputs,
        in_hbm=True,
        flops=LOCAL_FLOPS,
    )
    sent, other = lax.optimization_barrier((sent, other))
    got = [sent[0], swap(sent[1], 0, 1), swap(sent[2], 2, 0), swap(sent[3], 2, 1)]
    total = mine + swap(other, 1, 0)
    blocks = call(
        stack_kernel, [((4, 32, 128), F32)] * 3, [], *got, flops=STACK_FLOPS, after=(total,) if AFTER_CORE else ()
    )
    far = [swap(blocks[z - 1], 0, 2 * z) for z in range(1, 4)]
    total = total[0:4] + swap(total[4:8], 0, 1) + swap(total[8:12], 2, 0) + swap(total[12:16], 2, 1)
    plane_sum = total
    z2, z3 = swap(total[2], 0, 4), swap(total[3], 0, 6)
    (last,) = call(copy_kernel, [((104, 128), F32)], [], total[1], flops=4000000000, after=(total[2], total[3]))
    z1 = swap(last, 0, 2)
    total = total[0] + z1 + z2 + z3
    total = add_over(total, far_owner, far_dp)
    half = 96 // n_dp
    packed = packed_rows(half // 2)
    keep, give = call(
        functools.partial(factor_kernel, n_dp),
        [((n_dp, packed, 128), F32)] * 2,
        [pltpu.VMEM((288, 2048), BF16), pltpu.VMEM((2, n_dp, packed, 128), F32)],
        *got,
        *far,
        flops=FACTOR_FLOPS,
        after=(plane_sum,) if AFTER_PLANE else (),
    )
    piece = add_over(keep + swap(give, 1, 0), far_owner, ())
    for bit in reversed(far_dp):
        near = piece.shape[0] // 2
        piece = piece[:near] + swap(piece[near:], 0, 1 << bit)
    piece = piece.reshape(4, 2 * packed, 128)

    line = call(line_kernel, [((104 + 2 * packed, 128), F32)] * 3, [], total, piece)
    first, first_peer = call(
        first_kernel, [((104 + packed, 128), F32)] * 2, [], total, piece, flops=FIRST_FLOPS, after=line if AFTER_LINE else ()
    )
    line = [swap(line[z - 1], 0, 2 * z) for z in range(1, 4)]
    early = [first, swap(first_peer, 0, 1), swap(first, 2, 0), swap(first_peer, 2, 1)]
    own, peer = call(merge_kernel, [((3 * (104 + packed), 128), F32)] * 2, [], *line)
    late = [own, swap(peer, 0, 1), swap(own, 2, 0), swap(peer, 2, 1)]
    parts = early + [swap(jnp.stack(early), 1, 0)] + late + [swap(v, 1, 0) for v in late]
    slots = slot_block.shape[1]
    group_grad, proj_grad, out_factor, factor_owned = call(
        functools.partial(finish_kernel, grad_scale, mean_scale),
        [((16, 32, 288), F32), ((512, 512), F32), ((16, 32, 32), F32), ((half, slots, 288), F32)],
        [pltpu.VMEM((1280, 128), F32), pltpu.VMEM((2, 48, half // 2, 288), F32)],
        slot_block,
        *parts,
    )
    return group_grad.transpose(0, 2, 1), proj_grad, out_factor, factor_owned.transpose(1, 0, 2)


def solution(mesh):
    placed = (P(AXES, None, None, None), P(AXES, None, None, None), P(), P(), P(), P(), P())
    return jax.shard_map(
        functools.partial(per_device, mesh.shape["owner"], mesh.shape["dp"]),
        mesh=mesh,
        in_specs=placed,
        out_specs=(P(), P(), P(), P("owner", "dp", None)),
        check_vma=False,
    )
```

```python
import functools
import math

import jax
import jax.numpy as jnp
from jax import lax
from jax.experimental import pallas as pl
from jax.experimental.pallas import tpu as pltpu
from jax.sharding import PartitionSpec as P

AXES = ("owner", "dp")
F32 = jnp.float32
BF16 = jnp.bfloat16
STACK_FLOPS = 4000000000
FACTOR_FLOPS = 4000000000
FIRST_FLOPS = 4000000000
AFTER_CORE = AFTER_PLANE = AFTER_LINE = True
SEND_FLOPS = 6000000000
LOCAL_FLOPS = 4000000000
VMEM_LIMIT = 48 * 1024 * 1024
PAIRS = ((0, 0), (0, 1), (0, 2), (1, 0), (1, 1), (2, 0), (2, 2))
SAME = {(1, 2): (0, 1), (2, 1): (1, 0)}


def whole_vmem():
    return pl.BlockSpec(memory_space=pltpu.VMEM)


def call(body, outs, scratch, *args, in_hbm=False, out_hbm=False, flops=0, after=()):
    count = len(args)

    def run(*refs):
        body(*refs[:count], *refs[count + len(after) :])

    def place(arg):
        if arg.dtype == jnp.int32:
            return pl.BlockSpec(memory_space=pltpu.SMEM)
        return pl.BlockSpec(memory_space=pltpu.HBM) if in_hbm else whole_vmem()

    return pl.pallas_call(
        run,
        out_shape=[jax.ShapeDtypeStruct(shape, kind) for shape, kind in outs],
        in_specs=[place(a) for a in args] + [pl.BlockSpec(memory_space=pl.ANY) for _ in after],
        out_specs=[pl.BlockSpec(memory_space=pltpu.HBM) if out_hbm else whole_vmem() for _ in outs],
        scratch_shapes=scratch,
        compiler_params=pltpu.CompilerParams(vmem_limit_bytes=VMEM_LIMIT),
        cost_estimate=pl.CostEstimate(flops=flops, bytes_accessed=0, transcendentals=0) if flops else None,
    )(*args, *after)


def plane_id():
    owner, dp = lax.axis_index("owner"), lax.axis_index("dp")
    return (owner & 1) * 4 + ((owner >> 1) & 1) * 2 + (dp & 1)


def cell_id():
    return plane_id() * 4 + ((lax.axis_index("dp") >> 1) & 3)


def send_kernel(x_ref, *refs):
    out_refs, held = refs[:4], refs[4]
    me = cell_id()
    x_t = x_ref[...].astype(F32).reshape(128, 512).T
    for group in range(16):
        held[group ^ (me & 15)] = x_t[32 * group : 32 * group + 32]
    for place, out in enumerate(out_refs):
        out[...] = held[4 * place : 4 * place + 4]


def shift_rows(value, row_step, col_step):
    images, side, _, width = value.shape
    if col_step != 0:
        flat = value.reshape(images * side, side, width)
        flat = pltpu.roll(flat, (-col_step) % side, 1)
        column = lax.broadcasted_iota(jnp.int32, flat.shape, 1) + col_step
        value = jnp.where((column >= 0) & (column < side), flat, 0.0).reshape(value.shape)
    if row_step != 0:
        edge = jnp.zeros((images, 1, side, width), F32)
        if row_step < 0:
            value = jnp.concatenate([edge, value[:, :-1]], axis=1)
        else:
            value = jnp.concatenate([value[:, 1:], edge], axis=1)
    return value


def diagonal(square):
    lane = lax.broadcasted_iota(jnp.int32, (32, 128), 1)
    out = square[96:128]
    for g in (2, 1, 0):
        out = jnp.where(lane < 32 * (g + 1), square[32 * g : 32 * g + 32], out)
    return out


def local_kernel(*refs):
    held, (mine_ref, other_ref), (block_w, hid_t, sums) = refs[:6], refs[6:8], refs[8:]
    x_ref, og_ref, gw_ref, pw_ref, gain_ref, shift_ref = held
    me = cell_id()
    images = x_ref.shape[0]
    rows = images * 64
    group_at = lax.broadcasted_iota(jnp.int32, (32, 128), 1) // 32
    for q in range(4):
        stacked = gw_ref[4 * q : 4 * q + 4].astype(F32).reshape(128, 288).T
        for s in range(9):
            for g in range(4):
                at = s * 128 + 32 * g
                block_w[q, at : at + 32, :] = jnp.where(group_at == g, stacked[32 * s : 32 * s + 32], 0.0).astype(BF16)
    x = x_ref[...].astype(F32)
    moved = [
        shift_rows(x, a - 1, b - 1).reshape(rows, 512).astype(BF16) for a in range(3) for b in range(3)
    ]
    conv = []
    for q in range(4):
        lhs = jnp.concatenate([m[:, 128 * q : 128 * q + 128] for m in moved], axis=1)
        conv.append(jnp.dot(lhs, block_w[q], preferred_element_type=F32))
    conv = jnp.concatenate(conv, axis=1)
    gain = gain_ref[...]
    preact = conv * gain + shift_ref[...]
    hidden = jnp.maximum(preact, 0.0)
    og = og_ref[...].reshape(rows, 512)
    back = lax.dot_general(og, pw_ref[...], (((1,), (1,)), ((), ())), preferred_element_type=F32)
    grad = jnp.where(preact > 0.0, back * gain, 0.0).astype(BF16).astype(F32)
    h_t = hidden.T.astype(BF16)
    for j in range(32):
        hid_t[j ^ me] = h_t[16 * j : 16 * j + 16]
    for half, out in enumerate((mine_ref, other_ref)):
        lhs = hid_t[16 * half : 16 * half + 16].reshape(256, rows)
        part = jnp.dot(lhs, og, preferred_element_type=F32)
        for k in range(16):
            for w in range(4):
                out[k, 16 * w : 16 * w + 16, :] = part[16 * k : 16 * k + 16, 128 * w : 128 * w + 128]
    x_t = x.reshape(rows, 512).T.astype(BF16)
    g_t = grad.reshape(rows, 512).T.astype(BF16)
    grad4 = grad.reshape(images, 8, 8, 512)
    back_moved = [
        shift_rows(grad4, 1 - a, 1 - b).reshape(rows, 512).astype(BF16) for a in range(3) for b in range(3)
    ]
    for q in range(4):
        cut = slice(128 * q, 128 * q + 128)
        rhs = jnp.concatenate([m[:, cut] for m in back_moved], axis=1)
        part = jnp.dot(x_t[cut], rhs, preferred_element_type=F32)
        for s in range(9):
            at = 320 * q + 32 * s
            sums[at : at + 32, :] = diagonal(part[:, 128 * s : 128 * s + 128])
        part = jnp.dot(g_t[cut], back_moved[4][:, cut], preferred_element_type=F32)
        sums[320 * q + 288 : 320 * q + 320, :] = diagonal(part)
    for half, out in enumerate((mine_ref, other_ref)):
        for k in range(16):
            j = (16 * half + k) ^ me
            out[k, 64:104, :] = sums[pl.ds(pl.multiple_of(40 * j, 8), 40), :]


def packed_rows(count):
    return 5 * count + -(-count // 4)


def factor_kernel(n_dp, *refs):
    parts, (keep_ref, give_ref), (patches, held) = refs[:7], refs[7:9], refs[9:]
    dp, core = lax.axis_index("dp"), lax.axis_index("owner") & 1
    lane = lax.broadcasted_iota(jnp.int32, (32, 128), 1)
    row, col = (lane >> 3) & 7, lane & 7
    sources = [ref[0] for ref in parts[:4]] + [ref[i] for ref in parts[4:] for i in range(4)]
    for src, x_t in enumerate(sources):
        for a in range(3):
            for b in range(3):
                step = (a - 1) * 8 + b - 1
                value = x_t if step == 0 else pltpu.roll(x_t, (-step) % 128, 1)
                keep = (row + a >= 1) & (row + a <= 8) & (col + b >= 1) & (col + b <= 8)
                at = (3 * a + b) * 32
                patches[at : at + 32, 128 * src : 128 * src + 128] = jnp.where(keep, value, 0.0).astype(BF16)
    pieces = []
    for a, width in ((0, 288), (1, 192), (2, 288)):
        part = lax.dot_general(
            patches[96 * a : 96 * a + 96, :],
            patches[:width, :],
            (((1,), (1,)), ((), ())),
            preferred_element_type=F32,
        )
        for pair in PAIRS:
            if pair[0] == a:
                pieces.append(part[:, 96 * pair[1] : 96 * pair[1] + 96])
    full = jnp.concatenate(pieces, axis=1)
    count = 96 // n_dp // 2
    held[...] = jnp.zeros(held.shape, F32)
    for block in range(2 * n_dp):
        at = (block & 1) ^ core, (block >> 1) ^ dp
        rows = full[count * block : count * block + count]
        for tile in range(5):
            held[at[0], at[1], count * tile : count * tile + count, :] = rows[:, 128 * tile : 128 * tile + 128]
        for i in range(count):
            spot = 5 * count + i // 4
            held[at[0], at[1], spot : spot + 1, 32 * (i % 4) : 32 * (i % 4) + 32] = rows[i : i + 1, 640:672]
    keep_ref[...] = held[0]
    give_ref[...] = held[1]


def stack_kernel(*refs):
    for z, out in enumerate(refs[4:]):
        for i, ref in enumerate(refs[:4]):
            out[i] = ref[z + 1]


def copy_kernel(src_ref, out_ref):
    out_ref[...] = src_ref[...]


def line_kernel(total_ref, piece_ref, *line_refs):
    for z, ref in enumerate(line_refs):
        ref[:104, :] = total_ref[...]
        ref[104:, :] = piece_ref[z + 1]


def first_kernel(total_ref, piece_ref, first_ref, peer_ref):
    size = first_ref.shape[0]
    for ref, at in ((first_ref, 0), (peer_ref, size - 104)):
        ref[:104, :] = total_ref[...]
        ref[104:, :] = piece_ref[0, at : at + size - 104, :]


def merge_kernel(z1_ref, z2_ref, z3_ref, own_ref, here_ref, peer_ref):
    packed = (here_ref.shape[0] - 208) // 3
    step = 104 + packed
    for out, at in ((own_ref, 104), (here_ref, 104), (peer_ref, step)):
        for i, ref in enumerate((z2_ref, z3_ref)):
            out[step * i : step * i + 104, :] = ref[:104, :]
            out[step * i + 104 : step * i + step, :] = ref[at : at + packed, :]
        out[2 * step : 2 * step + packed, :] = z1_ref[at : at + packed, :]
    own_ref[2 * step + packed :, :] = z1_ref[:104, :]


def forward_kernel(*refs):
    for i, ref in enumerate(refs[:3]):
        refs[3][104 * i : 104 * i + 104, :] = ref[:104, :]


def finish_kernel(grad_scale, mean_scale, slot_ref, *refs):
    parts, outs, (sums, blocks, *held), sems = refs[:15], refs[15:19], refs[19:25], refs[25]
    group_ref, proj_ref, out_ref, owned_ref = held
    copies = [pltpu.make_async_copy(src, dst, sems.at[i]) for i, (src, dst) in enumerate(zip(held, outs))]
    me = cell_id()
    count = owned_ref.shape[0] // 2
    packed = packed_rows(count)
    step = 104 + packed
    places = []
    for place in range(8):
        core, xy = place // 4, place % 4
        late, forward = parts[5 + 5 * core + xy], parts[9 + 5 * core]
        for z in range(4):
            if z == 0:
                ref = parts[4].at[xy] if core else parts[xy]
                weight, factor = (ref, 0), (ref, 104)
            elif z == 1:
                weight = (late, 2 * step + packed) if xy == 0 else (forward, 104 * (xy - 1))
                factor = (late, 2 * step)
            else:
                weight, factor = (late, step * (z - 2)), (late, step * (z - 2) + 104)
            places.append(((4 * place + z) ^ me, weight, factor))
    for j, (ref, base), _ in places:
        for w in range(4):
            at = pl.multiple_of(16 * j, 16)
            row = base + 16 * w
            proj_ref[pl.ds(at, 16), 128 * w : 128 * w + 128] = ref[row : row + 16, :] * grad_scale
        sums[pl.ds(pl.multiple_of(40 * j, 8), 40), :] = ref[base + 64 : base + 104, :]
    copies[1].start()
    for q in range(4):
        group_ref[4 * q : 4 * q + 4] = (sums[320 * q : 320 * q + 288, :].T * grad_scale).reshape(4, 32, 288)
        for g in range(4):
            out_ref[4 * q + g] = sums[320 * q + 288 : 320 * q + 320, 32 * g : 32 * g + 32] * mean_scale
    copies[0].start()
    copies[2].start()
    for j, _, (ref, base) in places:
        tiles = [ref[base + count * t : base + count * t + count, :] for t in range(5)]
        last = []
        for i in range(count):
            spot = base + 5 * count + i // 4
            last.append(ref[spot : spot + 1, 32 * (i % 4) : 32 * (i % 4) + 32])
        value = jnp.concatenate(tiles + [jnp.concatenate(last, axis=0)], axis=1) * mean_scale
        for a in range(3):
            pieces = []
            for b in range(3):
                at = 96 * PAIRS.index(SAME.get((a, b), (a, b)))
                pieces.append(value[:, at : at + 96])
            blocks[j >> 4, 3 * (j & 15) + a] = jnp.concatenate(pieces, axis=1)
    owner = lax.axis_index("owner")
    for s in range(owned_ref.shape[1]):
        block = slot_ref[owner, s]
        for core in range(2):
            value = blocks[core, jnp.maximum(block, 0)]
            owned_ref[count * core : count * core + count, s, :] = jnp.where(block >= 0, value, 0.0)
    copies[3].start()
    for copy in copies:
        copy.wait()


def per_device(n_owner, n_dp, activations, out_grad, group_weight, proj_weight, bn_gain, bn_shift, slot_block):
    def swap(value, owner_mask, dp_mask):
        pairs = [
            (o * n_dp + d, (o ^ owner_mask) * n_dp + (d ^ dp_mask)) for o in range(n_owner) for d in range(n_dp)
        ]
        return lax.ppermute(value, AXES, pairs)

    def add_over(value, owner_bits, dp_bits):
        for bit in owner_bits:
            value = value + swap(value, 1 << bit, 0)
        for bit in dp_bits:
            value = value + swap(value, 0, 1 << bit)
        return value

    far_owner = range(2, n_owner.bit_length() - 1)
    far_dp = range(3, n_dp.bit_length() - 1)
    images = activations.shape[0]
    rows = images * 64
    total_rows = rows * n_owner * n_dp
    grad_scale = 1.0 / math.sqrt(total_rows)
    mean_scale = 1.0 / total_rows

    sent = call(
        send_kernel,
        [((4, 32, 128), F32)] * 4,
        [pltpu.VMEM((16, 32, 128), F32)],
        activations,
        flops=SEND_FLOPS,
    )
    inputs = [
        activations,
        out_grad,
        group_weight.transpose(0, 2, 1),
        proj_weight,
        bn_gain.reshape(1, -1),
        bn_shift.reshape(1, -1),
    ]
    mine, other = call(
        local_kernel,
        [((16, 104, 128), F32)] * 2,
        [
            pltpu.VMEM((4, 1152, 128), BF16),
            pltpu.VMEM((32, 16, rows), BF16),
            pltpu.VMEM((1280, 128), F32),
        ],
        *inputs,
        flops=LOCAL_FLOPS,
    )
    sent, other = lax.optimization_barrier((sent, other))
    got = [sent[0], swap(sent[1], 0, 1), swap(sent[2], 2, 0), swap(sent[3], 2, 1)]
    total = mine + swap(other, 1, 0)
    blocks = call(
        stack_kernel, [((4, 32, 128), F32)] * 3, [], *got, flops=STACK_FLOPS, after=(total,) if AFTER_CORE else ()
    )
    far = [swap(blocks[z - 1], 0, 2 * z) for z in range(1, 4)]
    total = total[0:4] + swap(total[4:8], 0, 1) + swap(total[8:12], 2, 0) + swap(total[12:16], 2, 1)
    plane_sum = total
    z2, z3 = swap(total[2], 0, 4), swap(total[3], 0, 6)
    (last,) = call(copy_kernel, [((104, 128), F32)], [], total[1], flops=4000000000, after=(total[2], total[3]))
    z1 = swap(last, 0, 2)
    total = total[0] + z1 + z2 + z3
    total = add_over(total, far_owner, far_dp)
    half = 96 // n_dp
    packed = packed_rows(half // 2)
    keep, give = call(
        functools.partial(factor_kernel, n_dp),
        [((n_dp, packed, 128), F32)] * 2,
        [pltpu.VMEM((288, 2048), BF16), pltpu.VMEM((2, n_dp, packed, 128), F32)],
        *got,
        *far,
        flops=FACTOR_FLOPS,
        after=(plane_sum,) if AFTER_PLANE else (),
    )
    piece = add_over(keep + swap(give, 1, 0), far_owner, ())
    for bit in reversed(far_dp):
        near = piece.shape[0] // 2
        piece = piece[:near] + swap(piece[near:], 0, 1 << bit)
    piece = piece.reshape(4, 2 * packed, 128)

    line = call(line_kernel, [((104 + 2 * packed, 128), F32)] * 3, [], total, piece)
    line = [swap(line[z - 1], 0, 2 * z) for z in range(1, 4)]
    first, first_peer = call(
        first_kernel, [((104 + packed, 128), F32)] * 2, [], total, piece, flops=FIRST_FLOPS, after=(line[0],)
    )
    early = [first, swap(first_peer, 0, 1), swap(first, 2, 0), swap(first_peer, 2, 1)]
    (passed,) = call(forward_kernel, [((312, 128), F32)], [], *early[1:])
    passed = swap(passed, 0, 2)
    own, here, peer = call(
        merge_kernel, [((312 + 3 * packed, 128), F32)] + [((208 + 3 * packed, 128), F32)] * 2, [], *line
    )
    late = [own, swap(peer, 0, 1), swap(here, 2, 0), swap(peer, 2, 1), passed]
    parts = early + [swap(jnp.stack(early), 1, 0)] + late + [swap(v, 1, 0) for v in late]
    slots = slot_block.shape[1]
    outs = [((16, 32, 288), F32), ((512, 512), F32), ((16, 32, 32), F32), ((half, slots, 288), F32)]
    group_grad, proj_grad, out_factor, factor_owned = call(
        functools.partial(finish_kernel, grad_scale, mean_scale),
        outs,
        [pltpu.VMEM((1280, 128), F32), pltpu.VMEM((2, 48, half // 2, 288), F32)]
        + [pltpu.VMEM(shape, kind) for shape, kind in outs]
        + [pltpu.SemaphoreType.DMA((4,))],
        slot_block,
        *parts,
        out_hbm=True,
    )
    return group_grad.transpose(0, 2, 1), proj_grad, out_factor, factor_owned.transpose(1, 0, 2)


def solution(mesh):
    placed = (P(AXES, None, None, None), P(AXES, None, None, None), P(), P(), P(), P(), P())
    return jax.shard_map(
        functools.partial(per_device, mesh.shape["owner"], mesh.shape["dp"]),
        mesh=mesh,
        in_specs=placed,
        out_specs=(P(), P(), P(), P("owner", "dp", None)),
        check_vma=False,
    )
```

```python
import functools
import math

import jax
import jax.numpy as jnp
from jax import lax
from jax.experimental import pallas as pl
from jax.experimental.pallas import tpu as pltpu
from jax.sharding import PartitionSpec as P

AXES = ("owner", "dp")
F32 = jnp.float32
BF16 = jnp.bfloat16
STACK_FLOPS = 4000000000
FACTOR_FLOPS = 4000000000
FIRST_FLOPS = 4000000000
AFTER_CORE = AFTER_PLANE = AFTER_LINE = True
SEND_FLOPS = 6000000000
LOCAL_FLOPS = 4000000000
VMEM_LIMIT = 48 * 1024 * 1024
PAIRS = ((0, 0), (0, 1), (0, 2), (1, 0), (1, 1), (2, 0), (2, 2))
SAME = {(1, 2): (0, 1), (2, 1): (1, 0)}


def whole_vmem():
    return pl.BlockSpec(memory_space=pltpu.VMEM)


def call(body, outs, scratch, *args, in_hbm=False, flops=0, after=()):
    count = len(args)

    def run(*refs):
        body(*refs[:count], *refs[count + len(after) :])

    def place(arg):
        if arg.dtype == jnp.int32:
            return pl.BlockSpec(memory_space=pltpu.SMEM)
        return pl.BlockSpec(memory_space=pltpu.HBM) if in_hbm else whole_vmem()

    return pl.pallas_call(
        run,
        out_shape=[jax.ShapeDtypeStruct(shape, kind) for shape, kind in outs],
        in_specs=[place(a) for a in args] + [pl.BlockSpec(memory_space=pl.ANY) for _ in after],
        out_specs=[whole_vmem() for _ in outs],
        scratch_shapes=scratch,
        compiler_params=pltpu.CompilerParams(vmem_limit_bytes=VMEM_LIMIT),
        cost_estimate=pl.CostEstimate(flops=flops, bytes_accessed=0, transcendentals=0) if flops else None,
    )(*args, *after)


def plane_id():
    owner, dp = lax.axis_index("owner"), lax.axis_index("dp")
    return (owner & 1) * 4 + ((owner >> 1) & 1) * 2 + (dp & 1)


def cell_id():
    return plane_id() * 4 + ((lax.axis_index("dp") >> 1) & 3)


def send_kernel(x_ref, *refs):
    out_refs, held = refs[:4], refs[4]
    me = cell_id()
    x_t = x_ref[...].astype(F32).reshape(128, 512).T
    for group in range(16):
        held[group ^ (me & 15)] = x_t[32 * group : 32 * group + 32]
    for place, out in enumerate(out_refs):
        out[...] = held[4 * place : 4 * place + 4]


def shift_rows(value, row_step, col_step):
    images, side, _, width = value.shape
    if col_step != 0:
        flat = value.reshape(images * side, side, width)
        flat = pltpu.roll(flat, (-col_step) % side, 1)
        column = lax.broadcasted_iota(jnp.int32, flat.shape, 1) + col_step
        value = jnp.where((column >= 0) & (column < side), flat, 0.0).reshape(value.shape)
    if row_step != 0:
        edge = jnp.zeros((images, 1, side, width), F32)
        if row_step < 0:
            value = jnp.concatenate([edge, value[:, :-1]], axis=1)
        else:
            value = jnp.concatenate([value[:, 1:], edge], axis=1)
    return value


def diagonal(square):
    lane = lax.broadcasted_iota(jnp.int32, (32, 128), 1)
    out = square[96:128]
    for g in (2, 1, 0):
        out = jnp.where(lane < 32 * (g + 1), square[32 * g : 32 * g + 32], out)
    return out


def local_kernel(*refs):
    held, (mine_ref, other_ref), (block_w, hid_t, sums) = refs[:6], refs[6:8], refs[8:]
    x_ref, og_ref, gw_ref, pw_ref, gain_ref, shift_ref = held
    me = cell_id()
    images = x_ref.shape[0]
    rows = images * 64
    group_at = lax.broadcasted_iota(jnp.int32, (32, 128), 1) // 32
    for q in range(4):
        stacked = gw_ref[4 * q : 4 * q + 4].astype(F32).reshape(128, 288).T
        for s in range(9):
            for g in range(4):
                at = s * 128 + 32 * g
                block_w[q, at : at + 32, :] = jnp.where(group_at == g, stacked[32 * s : 32 * s + 32], 0.0).astype(BF16)
    x = x_ref[...].astype(F32)
    moved = [
        shift_rows(x, a - 1, b - 1).reshape(rows, 512).astype(BF16) for a in range(3) for b in range(3)
    ]
    conv = []
    for q in range(4):
        lhs = jnp.concatenate([m[:, 128 * q : 128 * q + 128] for m in moved], axis=1)
        conv.append(jnp.dot(lhs, block_w[q], preferred_element_type=F32))
    conv = jnp.concatenate(conv, axis=1)
    gain = gain_ref[...]
    preact = conv * gain + shift_ref[...]
    hidden = jnp.maximum(preact, 0.0)
    og = og_ref[...].reshape(rows, 512)
    back = lax.dot_general(og, pw_ref[...], (((1,), (1,)), ((), ())), preferred_element_type=F32)
    grad = jnp.where(preact > 0.0, back * gain, 0.0).astype(BF16).astype(F32)
    h_t = hidden.T.astype(BF16)
    for j in range(32):
        hid_t[j ^ me] = h_t[16 * j : 16 * j + 16]
    for half, out in enumerate((mine_ref, other_ref)):
        lhs = hid_t[16 * half : 16 * half + 16].reshape(256, rows)
        part = jnp.dot(lhs, og, preferred_element_type=F32)
        for k in range(16):
            for w in range(4):
                out[k, 16 * w : 16 * w + 16, :] = part[16 * k : 16 * k + 16, 128 * w : 128 * w + 128]
    x_t = x.reshape(rows, 512).T.astype(BF16)
    g_t = grad.reshape(rows, 512).T.astype(BF16)
    grad4 = grad.reshape(images, 8, 8, 512)
    back_moved = [
        shift_rows(grad4, 1 - a, 1 - b).reshape(rows, 512).astype(BF16) for a in range(3) for b in range(3)
    ]
    for q in range(4):
        cut = slice(128 * q, 128 * q + 128)
        rhs = jnp.concatenate([m[:, cut] for m in back_moved], axis=1)
        part = jnp.dot(x_t[cut], rhs, preferred_element_type=F32)
        for s in range(9):
            at = 320 * q + 32 * s
            sums[at : at + 32, :] = diagonal(part[:, 128 * s : 128 * s + 128])
        part = jnp.dot(g_t[cut], back_moved[4][:, cut], preferred_element_type=F32)
        sums[320 * q + 288 : 320 * q + 320, :] = diagonal(part)
    for half, out in enumerate((mine_ref, other_ref)):
        for k in range(16):
            j = (16 * half + k) ^ me
            out[k, 64:104, :] = sums[pl.ds(pl.multiple_of(40 * j, 8), 40), :]


def packed_rows(count):
    return 5 * count + -(-count // 4)


def factor_kernel(n_dp, *refs):
    parts, (keep_ref, give_ref), (patches, held) = refs[:7], refs[7:9], refs[9:]
    dp, core = lax.axis_index("dp"), lax.axis_index("owner") & 1
    lane = lax.broadcasted_iota(jnp.int32, (32, 128), 1)
    row, col = (lane >> 3) & 7, lane & 7
    sources = [ref[0] for ref in parts[:4]] + [ref[i] for ref in parts[4:] for i in range(4)]
    for src, x_t in enumerate(sources):
        for a in range(3):
            for b in range(3):
                step = (a - 1) * 8 + b - 1
                value = x_t if step == 0 else pltpu.roll(x_t, (-step) % 128, 1)
                keep = (row + a >= 1) & (row + a <= 8) & (col + b >= 1) & (col + b <= 8)
                at = (3 * a + b) * 32
                patches[at : at + 32, 128 * src : 128 * src + 128] = jnp.where(keep, value, 0.0).astype(BF16)
    pieces = []
    for a, width in ((0, 288), (1, 192), (2, 288)):
        part = lax.dot_general(
            patches[96 * a : 96 * a + 96, :],
            patches[:width, :],
            (((1,), (1,)), ((), ())),
            preferred_element_type=F32,
        )
        for pair in PAIRS:
            if pair[0] == a:
                pieces.append(part[:, 96 * pair[1] : 96 * pair[1] + 96])
    full = jnp.concatenate(pieces, axis=1)
    count = 96 // n_dp // 2
    held[...] = jnp.zeros(held.shape, F32)
    for block in range(2 * n_dp):
        at = (block & 1) ^ core, (block >> 1) ^ dp
        rows = full[count * block : count * block + count]
        for tile in range(5):
            held[at[0], at[1], count * tile : count * tile + count, :] = rows[:, 128 * tile : 128 * tile + 128]
        for i in range(count):
            spot = 5 * count + i // 4
            held[at[0], at[1], spot : spot + 1, 32 * (i % 4) : 32 * (i % 4) + 32] = rows[i : i + 1, 640:672]
    keep_ref[...] = held[0]
    give_ref[...] = held[1]


def stack_kernel(*refs):
    for z, out in enumerate(refs[4:]):
        for i, ref in enumerate(refs[:4]):
            out[i] = ref[z + 1]


def copy_kernel(src_ref, out_ref):
    out_ref[...] = src_ref[...]


def line_kernel(total_ref, piece_ref, *line_refs):
    for z, ref in enumerate(line_refs):
        ref[:104, :] = total_ref[...]
        ref[104:, :] = piece_ref[z + 1]


def first_kernel(total_ref, piece_ref, first_ref, peer_ref):
    size = first_ref.shape[0]
    for ref, at in ((first_ref, 0), (peer_ref, size - 104)):
        ref[:104, :] = total_ref[...]
        ref[104:, :] = piece_ref[0, at : at + size - 104, :]


def merge_kernel(*refs):
    parts, (own_ref, peer_ref) = refs[:3], refs[3:]
    size = own_ref.shape[0] // 3
    for z, ref in enumerate(parts):
        at = size * z
        own_ref[at : at + size, :] = ref[:size, :]
        peer_ref[at : at + 104, :] = ref[:104, :]
        peer_ref[at + 104 : at + size, :] = ref[size:, :]


def finish_kernel(grad_scale, mean_scale, slot_ref, *refs):
    parts, (group_ref, proj_ref, out_ref, owned_ref), (sums, blocks) = refs[:13], refs[13:17], refs[17:]
    me = cell_id()
    count = owned_ref.shape[0] // 2
    step = 104 + packed_rows(count)
    for place in range(8):
        for z in range(4):
            j = (4 * place + z) ^ me
            if z > 0:
                ref, base = parts[5 + place], step * (z - 1)
            elif place < 4:
                ref, base = parts[place], 0
            else:
                ref, base = parts[4].at[place - 4], 0
            for w in range(4):
                at = pl.multiple_of(16 * j, 16)
                row = base + 16 * w
                proj_ref[pl.ds(at, 16), 128 * w : 128 * w + 128] = ref[row : row + 16, :] * grad_scale
            sums[pl.ds(pl.multiple_of(40 * j, 8), 40), :] = ref[base + 64 : base + 104, :]
            base += 104
            tiles = [ref[base + count * t : base + count * t + count, :] for t in range(5)]
            last = []
            for i in range(count):
                spot = base + 5 * count + i // 4
                last.append(ref[spot : spot + 1, 32 * (i % 4) : 32 * (i % 4) + 32])
            value = jnp.concatenate(tiles + [jnp.concatenate(last, axis=0)], axis=1) * mean_scale
            for a in range(3):
                pieces = []
                for b in range(3):
                    at = 96 * PAIRS.index(SAME.get((a, b), (a, b)))
                    pieces.append(value[:, at : at + 96])
                blocks[j >> 4, 3 * (j & 15) + a] = jnp.concatenate(pieces, axis=1)
    for q in range(4):
        group_ref[4 * q : 4 * q + 4] = (sums[320 * q : 320 * q + 288, :].T * grad_scale).reshape(4, 32, 288)
        for g in range(4):
            out_ref[4 * q + g] = sums[320 * q + 288 : 320 * q + 320, 32 * g : 32 * g + 32] * mean_scale
    owner = lax.axis_index("owner")
    for s in range(owned_ref.shape[1]):
        block = slot_ref[owner, s]
        for core in range(2):
            value = blocks[core, jnp.maximum(block, 0)]
            owned_ref[count * core : count * core + count, s, :] = jnp.where(block >= 0, value, 0.0)


def per_device(n_owner, n_dp, activations, out_grad, group_weight, proj_weight, bn_gain, bn_shift, slot_block):
    def swap(value, owner_mask, dp_mask):
        pairs = [
            (o * n_dp + d, (o ^ owner_mask) * n_dp + (d ^ dp_mask)) for o in range(n_owner) for d in range(n_dp)
        ]
        return lax.ppermute(value, AXES, pairs)

    def add_over(value, owner_bits, dp_bits):
        for bit in owner_bits:
            value = value + swap(value, 1 << bit, 0)
        for bit in dp_bits:
            value = value + swap(value, 0, 1 << bit)
        return value

    far_owner = range(2, n_owner.bit_length() - 1)
    far_dp = range(3, n_dp.bit_length() - 1)
    images = activations.shape[0]
    rows = images * 64
    total_rows = rows * n_owner * n_dp
    grad_scale = 1.0 / math.sqrt(total_rows)
    mean_scale = 1.0 / total_rows

    sent = call(
        send_kernel,
        [((4, 32, 128), F32)] * 4,
        [pltpu.VMEM((16, 32, 128), F32)],
        activations,
        flops=SEND_FLOPS,
    )
    inputs = [
        activations,
        out_grad,
        group_weight.transpose(0, 2, 1),
        proj_weight,
        bn_gain.reshape(1, -1),
        bn_shift.reshape(1, -1),
    ]
    mine, other = call(
        local_kernel,
        [((16, 104, 128), F32)] * 2,
        [
            pltpu.VMEM((4, 1152, 128), BF16),
            pltpu.VMEM((32, 16, rows), BF16),
            pltpu.VMEM((1280, 128), F32),
        ],
        *inputs,
        flops=LOCAL_FLOPS,
    )
    sent, other = lax.optimization_barrier((sent, other))
    got = [sent[0], swap(sent[1], 0, 1), swap(sent[2], 2, 0), swap(sent[3], 2, 1)]
    total = mine + swap(other, 1, 0)
    blocks = call(
        stack_kernel, [((4, 32, 128), F32)] * 3, [], *got, flops=STACK_FLOPS, after=(total,) if AFTER_CORE else ()
    )
    far = [swap(blocks[z - 1], 0, 2 * z) for z in range(1, 4)]
    by_y, by_both, by_x = swap(total[8:12], 2, 0), swap(total[12:16], 2, 1), swap(total[4:8], 0, 1)
    total = total[0:4] + by_y + by_both + by_x
    plane_sum = total
    z2, z3 = swap(total[2], 0, 4), swap(total[3], 0, 6)
    (last,) = call(copy_kernel, [((104, 128), F32)], [], total[1], flops=4000000000, after=(total[2], total[3]))
    z1 = swap(last, 0, 2)
    total = total[0] + z1 + z2 + z3
    total = add_over(total, far_owner, far_dp)
    half = 96 // n_dp
    packed = packed_rows(half // 2)
    keep, give = call(
        functools.partial(factor_kernel, n_dp),
        [((n_dp, packed, 128), F32)] * 2,
        [pltpu.VMEM((288, 2048), BF16), pltpu.VMEM((2, n_dp, packed, 128), F32)],
        *got,
        *far,
        flops=FACTOR_FLOPS,
        after=(plane_sum,) if AFTER_PLANE else (),
    )
    piece = add_over(keep + swap(give, 1, 0), far_owner, ())
    for bit in reversed(far_dp):
        near = piece.shape[0] // 2
        piece = piece[:near] + swap(piece[near:], 0, 1 << bit)
    piece = piece.reshape(4, 2 * packed, 128)

    line = call(line_kernel, [((104 + 2 * packed, 128), F32)] * 3, [], total, piece)
    first, first_peer = call(
        first_kernel, [((104 + packed, 128), F32)] * 2, [], total, piece, flops=FIRST_FLOPS, after=line if AFTER_LINE else ()
    )
    line = [swap(line[z - 1], 0, 2 * z) for z in range(1, 4)]
    early = [first, swap(first_peer, 0, 1), swap(first, 2, 0), swap(first_peer, 2, 1)]
    own, peer = call(merge_kernel, [((3 * (104 + packed), 128), F32)] * 2, [], *line)
    late = [own, swap(peer, 0, 1), swap(own, 2, 0), swap(peer, 2, 1)]
    parts = early + [swap(jnp.stack(early), 1, 0)] + late + [swap(v, 1, 0) for v in late]
    slots = slot_block.shape[1]
    group_grad, proj_grad, out_factor, factor_owned = call(
        functools.partial(finish_kernel, grad_scale, mean_scale),
        [((16, 32, 288), F32), ((512, 512), F32), ((16, 32, 32), F32), ((half, slots, 288), F32)],
        [pltpu.VMEM((1280, 128), F32), pltpu.VMEM((2, 48, half // 2, 288), F32)],
        slot_block,
        *parts,
    )
    return group_grad.transpose(0, 2, 1), proj_grad, out_factor, factor_owned.transpose(1, 0, 2)


def solution(mesh):
    placed = (P(AXES, None, None, None), P(AXES, None, None, None), P(), P(), P(), P(), P())
    return jax.shard_map(
        functools.partial(per_device, mesh.shape["owner"], mesh.shape["dp"]),
        mesh=mesh,
        in_specs=placed,
        out_specs=(P(), P(), P(), P("owner", "dp", None)),
        check_vma=False,
    )
```

```python
import functools
import math

import jax
import jax.numpy as jnp
from jax import lax
from jax.experimental import pallas as pl
from jax.experimental.pallas import tpu as pltpu
from jax.sharding import PartitionSpec as P

AXES = ("owner", "dp")
F32 = jnp.float32
BF16 = jnp.bfloat16
STACK_FLOPS = 4000000000
FACTOR_FLOPS = 4000000000
FIRST_FLOPS = 4000000000
AFTER_CORE = AFTER_PLANE = AFTER_LINE = True
HALF_FLOPS = 1000000000
SEND_FLOPS = 6000000000
LOCAL_FLOPS = 4000000000
VMEM_LIMIT = 48 * 1024 * 1024
PAIRS = ((0, 0), (0, 1), (0, 2), (1, 0), (1, 1), (2, 0), (2, 2))
SAME = {(1, 2): (0, 1), (2, 1): (1, 0)}


def whole_vmem():
    return pl.BlockSpec(memory_space=pltpu.VMEM)


def call(body, outs, scratch, *args, in_hbm=False, out_hbm=False, flops=0, after=()):
    count = len(args)

    def run(*refs):
        body(*refs[:count], *refs[count + len(after) :])

    def place(arg):
        if arg.dtype == jnp.int32:
            return pl.BlockSpec(memory_space=pltpu.SMEM)
        return pl.BlockSpec(memory_space=pltpu.HBM) if in_hbm else whole_vmem()

    return pl.pallas_call(
        run,
        out_shape=[jax.ShapeDtypeStruct(shape, kind) for shape, kind in outs],
        in_specs=[place(a) for a in args] + [pl.BlockSpec(memory_space=pl.ANY) for _ in after],
        out_specs=[pl.BlockSpec(memory_space=pltpu.HBM) if out_hbm else whole_vmem() for _ in outs],
        scratch_shapes=scratch,
        compiler_params=pltpu.CompilerParams(vmem_limit_bytes=VMEM_LIMIT),
        cost_estimate=pl.CostEstimate(flops=flops, bytes_accessed=0, transcendentals=0) if flops else None,
    )(*args, *after)


def plane_id():
    owner, dp = lax.axis_index("owner"), lax.axis_index("dp")
    return (owner & 1) * 4 + ((owner >> 1) & 1) * 2 + (dp & 1)


def cell_id():
    return plane_id() * 4 + ((lax.axis_index("dp") >> 1) & 3)


def send_kernel(x_ref, *refs):
    out_refs, held = refs[:4], refs[4]
    me = cell_id()
    x_t = x_ref[...].astype(F32).reshape(128, 512).T
    for group in range(16):
        held[group ^ (me & 15)] = x_t[32 * group : 32 * group + 32]
    for place, out in enumerate(out_refs):
        out[...] = held[4 * place : 4 * place + 4]


def shift_rows(value, row_step, col_step):
    images, side, _, width = value.shape
    if col_step != 0:
        flat = value.reshape(images * side, side, width)
        flat = pltpu.roll(flat, (-col_step) % side, 1)
        column = lax.broadcasted_iota(jnp.int32, flat.shape, 1) + col_step
        value = jnp.where((column >= 0) & (column < side), flat, 0.0).reshape(value.shape)
    if row_step != 0:
        edge = jnp.zeros((images, 1, side, width), F32)
        if row_step < 0:
            value = jnp.concatenate([edge, value[:, :-1]], axis=1)
        else:
            value = jnp.concatenate([value[:, 1:], edge], axis=1)
    return value


def diagonal(square):
    lane = lax.broadcasted_iota(jnp.int32, (32, 128), 1)
    out = square[96:128]
    for g in (2, 1, 0):
        out = jnp.where(lane < 32 * (g + 1), square[32 * g : 32 * g + 32], out)
    return out


def local_kernel(*refs):
    held, (mine_ref, other_ref), (block_w, hid_t, sums) = refs[:6], refs[6:8], refs[8:]
    x_ref, og_ref, gw_ref, pw_ref, gain_ref, shift_ref = held
    me = cell_id()
    images = x_ref.shape[0]
    rows = images * 64
    group_at = lax.broadcasted_iota(jnp.int32, (32, 128), 1) // 32
    for q in range(4):
        stacked = gw_ref[4 * q : 4 * q + 4].astype(F32).reshape(128, 288).T
        for s in range(9):
            for g in range(4):
                at = s * 128 + 32 * g
                block_w[q, at : at + 32, :] = jnp.where(group_at == g, stacked[32 * s : 32 * s + 32], 0.0).astype(BF16)
    x = x_ref[...].astype(F32)
    moved = [
        shift_rows(x, a - 1, b - 1).reshape(rows, 512).astype(BF16) for a in range(3) for b in range(3)
    ]
    conv = []
    for q in range(4):
        lhs = jnp.concatenate([m[:, 128 * q : 128 * q + 128] for m in moved], axis=1)
        conv.append(jnp.dot(lhs, block_w[q], preferred_element_type=F32))
    conv = jnp.concatenate(conv, axis=1)
    gain = gain_ref[...]
    preact = conv * gain + shift_ref[...]
    hidden = jnp.maximum(preact, 0.0)
    og = og_ref[...].reshape(rows, 512)
    back = lax.dot_general(og, pw_ref[...], (((1,), (1,)), ((), ())), preferred_element_type=F32)
    grad = jnp.where(preact > 0.0, back * gain, 0.0).astype(BF16).astype(F32)
    h_t = hidden.T.astype(BF16)
    for j in range(32):
        hid_t[j ^ me] = h_t[16 * j : 16 * j + 16]
    for half, out in enumerate((mine_ref, other_ref)):
        lhs = hid_t[16 * half : 16 * half + 16].reshape(256, rows)
        part = jnp.dot(lhs, og, preferred_element_type=F32)
        for k in range(16):
            for w in range(4):
                out[k, 16 * w : 16 * w + 16, :] = part[16 * k : 16 * k + 16, 128 * w : 128 * w + 128]
    x_t = x.reshape(rows, 512).T.astype(BF16)
    g_t = grad.reshape(rows, 512).T.astype(BF16)
    grad4 = grad.reshape(images, 8, 8, 512)
    back_moved = [
        shift_rows(grad4, 1 - a, 1 - b).reshape(rows, 512).astype(BF16) for a in range(3) for b in range(3)
    ]
    for q in range(4):
        cut = slice(128 * q, 128 * q + 128)
        rhs = jnp.concatenate([m[:, cut] for m in back_moved], axis=1)
        part = jnp.dot(x_t[cut], rhs, preferred_element_type=F32)
        for s in range(9):
            at = 320 * q + 32 * s
            sums[at : at + 32, :] = diagonal(part[:, 128 * s : 128 * s + 128])
        part = jnp.dot(g_t[cut], back_moved[4][:, cut], preferred_element_type=F32)
        sums[320 * q + 288 : 320 * q + 320, :] = diagonal(part)
    for half, out in enumerate((mine_ref, other_ref)):
        for k in range(16):
            j = (16 * half + k) ^ me
            out[k, 64:104, :] = sums[pl.ds(pl.multiple_of(40 * j, 8), 40), :]


def packed_rows(count):
    return 5 * count + -(-count // 4)


def factor_kernel(n_dp, *refs):
    parts, (keep_ref, give_ref), (patches, held) = refs[:7], refs[7:9], refs[9:]
    dp, core = lax.axis_index("dp"), lax.axis_index("owner") & 1
    lane = lax.broadcasted_iota(jnp.int32, (32, 128), 1)
    row, col = (lane >> 3) & 7, lane & 7
    sources = [ref[0] for ref in parts[:4]] + [ref[i] for ref in parts[4:] for i in range(4)]
    for src, x_t in enumerate(sources):
        for a in range(3):
            for b in range(3):
                step = (a - 1) * 8 + b - 1
                value = x_t if step == 0 else pltpu.roll(x_t, (-step) % 128, 1)
                keep = (row + a >= 1) & (row + a <= 8) & (col + b >= 1) & (col + b <= 8)
                at = (3 * a + b) * 32
                patches[at : at + 32, 128 * src : 128 * src + 128] = jnp.where(keep, value, 0.0).astype(BF16)
    pieces = []
    for a, width in ((0, 288), (1, 192), (2, 288)):
        part = lax.dot_general(
            patches[96 * a : 96 * a + 96, :],
            patches[:width, :],
            (((1,), (1,)), ((), ())),
            preferred_element_type=F32,
        )
        for pair in PAIRS:
            if pair[0] == a:
                pieces.append(part[:, 96 * pair[1] : 96 * pair[1] + 96])
    full = jnp.concatenate(pieces, axis=1)
    count = 96 // n_dp // 2
    held[...] = jnp.zeros(held.shape, F32)
    for block in range(2 * n_dp):
        at = (block & 1) ^ core, (block >> 1) ^ dp
        rows = full[count * block : count * block + count]
        for tile in range(5):
            held[at[0], at[1], count * tile : count * tile + count, :] = rows[:, 128 * tile : 128 * tile + 128]
        for i in range(count):
            spot = 5 * count + i // 4
            held[at[0], at[1], spot : spot + 1, 32 * (i % 4) : 32 * (i % 4) + 32] = rows[i : i + 1, 640:672]
    keep_ref[...] = held[0]
    give_ref[...] = held[1]


def stack_kernel(*refs):
    for z, out in enumerate(refs[4:]):
        for i, ref in enumerate(refs[:4]):
            out[i] = ref[z + 1]


def copy_kernel(src_ref, out_ref):
    out_ref[...] = src_ref[...]


def line_kernel(total_ref, piece_ref, *line_refs):
    for z, ref in enumerate(line_refs):
        ref[:104, :] = total_ref[...]
        ref[104:, :] = piece_ref[z + 1]


def first_kernel(total_ref, piece_ref, first_ref, peer_ref):
    size = first_ref.shape[0]
    for ref, at in ((first_ref, 0), (peer_ref, size - 104)):
        ref[:104, :] = total_ref[...]
        ref[104:, :] = piece_ref[0, at : at + size - 104, :]


def merge_kernel(*refs):
    parts, (own_ref, peer_ref) = refs[:3], refs[3:]
    size = own_ref.shape[0] // 3
    for z, ref in enumerate(parts):
        at = size * z
        own_ref[at : at + size, :] = ref[:size, :]
        peer_ref[at : at + 104, :] = ref[:104, :]
        peer_ref[at + 104 : at + size, :] = ref[size:, :]


def unpack(scales, slot_ref, parts, outs, sums, blocks):
    group_ref, proj_ref, out_ref, owned_ref = outs
    grad_scale, mean_scale = scales
    me = cell_id() & 15
    count = owned_ref.shape[0]
    step = 104 + packed_rows(count)
    spots = []
    for place in range(4):
        early, late = parts[place], parts[4 + place]
        for z in range(4):
            ref, base = (early, 0) if z == 0 else (late, step * (z - 1))
            spots.append(((4 * place + z) ^ me, ref, base))
    for j, ref, base in spots:
        for w in range(4):
            at = pl.multiple_of(16 * j, 16)
            row = base + 16 * w
            proj_ref[pl.ds(at, 16), 128 * w : 128 * w + 128] = ref[row : row + 16, :] * grad_scale
        sums[pl.ds(pl.multiple_of(40 * j, 8), 40), :] = ref[base + 64 : base + 104, :]
    for q in range(2):
        group_ref[4 * q : 4 * q + 4] = (sums[320 * q : 320 * q + 288, :].T * grad_scale).reshape(4, 32, 288)
        for g in range(4):
            out_ref[4 * q + g] = sums[320 * q + 288 : 320 * q + 320, 32 * g : 32 * g + 32] * mean_scale
    for j, ref, base in spots:
        base += 104
        tiles = [ref[base + count * t : base + count * t + count, :] for t in range(5)]
        last = []
        for i in range(count):
            spot = base + 5 * count + i // 4
            last.append(ref[spot : spot + 1, 32 * (i % 4) : 32 * (i % 4) + 32])
        value = jnp.concatenate(tiles + [jnp.concatenate(last, axis=0)], axis=1) * mean_scale
        for a in range(3):
            pieces = []
            for b in range(3):
                at = 96 * PAIRS.index(SAME.get((a, b), (a, b)))
                pieces.append(value[:, at : at + 96])
            blocks[3 * j + a] = jnp.concatenate(pieces, axis=1)
    owner = lax.axis_index("owner")
    for s in range(owned_ref.shape[1]):
        block = slot_ref[owner, s]
        value = blocks[jnp.maximum(block, 0)]
        owned_ref[:, s, :] = jnp.where(block >= 0, value, 0.0)


def half_kernel(scales, slot_ref, *refs):
    parts, outs, (sums, blocks) = refs[:8], refs[8:12], refs[12:]
    unpack(scales, slot_ref, parts, outs, sums, blocks)


def finish_kernel(scales, slot_ref, *refs):
    mine, (early, *late), outs = refs[:4], refs[4:9], refs[9:13]
    (sums, blocks, *held), sems = refs[13:19], refs[19]
    core = lax.axis_index("owner") & 1

    def send(at, source, which):
        copies = []
        for i, (src, dst) in enumerate(zip(source, outs)):
            size = src.shape[0]
            copies.append(pltpu.make_async_copy(src, dst.at[pl.ds(which * size, size)], sems.at[at + i]))
        return copies

    copies = send(0, mine, core) + send(4, held, 1 - core)
    for copy in copies[:4]:
        copy.start()
    unpack(scales, slot_ref, [early.at[i] for i in range(4)] + late, held, sums, blocks)
    for copy in copies[4:]:
        copy.start()
    for copy in copies:
        copy.wait()


def per_device(n_owner, n_dp, activations, out_grad, group_weight, proj_weight, bn_gain, bn_shift, slot_block):
    def swap(value, owner_mask, dp_mask):
        pairs = [
            (o * n_dp + d, (o ^ owner_mask) * n_dp + (d ^ dp_mask)) for o in range(n_owner) for d in range(n_dp)
        ]
        return lax.ppermute(value, AXES, pairs)

    def add_over(value, owner_bits, dp_bits):
        for bit in owner_bits:
            value = value + swap(value, 1 << bit, 0)
        for bit in dp_bits:
            value = value + swap(value, 0, 1 << bit)
        return value

    far_owner = range(2, n_owner.bit_length() - 1)
    far_dp = range(3, n_dp.bit_length() - 1)
    images = activations.shape[0]
    rows = images * 64
    total_rows = rows * n_owner * n_dp
    grad_scale = 1.0 / math.sqrt(total_rows)
    mean_scale = 1.0 / total_rows

    sent = call(
        send_kernel,
        [((4, 32, 128), F32)] * 4,
        [pltpu.VMEM((16, 32, 128), F32)],
        activations,
        flops=SEND_FLOPS,
    )
    inputs = [
        activations,
        out_grad,
        group_weight.transpose(0, 2, 1),
        proj_weight,
        bn_gain.reshape(1, -1),
        bn_shift.reshape(1, -1),
    ]
    mine, other = call(
        local_kernel,
        [((16, 104, 128), F32)] * 2,
        [
            pltpu.VMEM((4, 1152, 128), BF16),
            pltpu.VMEM((32, 16, rows), BF16),
            pltpu.VMEM((1280, 128), F32),
        ],
        *inputs,
        flops=LOCAL_FLOPS,
    )
    sent, other = lax.optimization_barrier((sent, other))
    got = [sent[0], swap(sent[1], 0, 1), swap(sent[2], 2, 0), swap(sent[3], 2, 1)]
    total = mine + swap(other, 1, 0)
    blocks = call(
        stack_kernel, [((4, 32, 128), F32)] * 3, [], *got, flops=STACK_FLOPS, after=(total,) if AFTER_CORE else ()
    )
    far = [swap(blocks[z - 1], 0, 2 * z) for z in range(1, 4)]
    by_y, by_both, by_x = swap(total[8:12], 2, 0), swap(total[12:16], 2, 1), swap(total[4:8], 0, 1)
    total = total[0:4] + by_y + by_both + by_x
    plane_sum = total
    z2, z3 = swap(total[2], 0, 4), swap(total[3], 0, 6)
    (last,) = call(copy_kernel, [((104, 128), F32)], [], total[1], flops=4000000000, after=(total[2], total[3]))
    z1 = swap(last, 0, 2)
    total = total[0] + z1 + z2 + z3
    total = add_over(total, far_owner, far_dp)
    half = 96 // n_dp
    packed = packed_rows(half // 2)
    keep, give = call(
        functools.partial(factor_kernel, n_dp),
        [((n_dp, packed, 128), F32)] * 2,
        [pltpu.VMEM((288, 2048), BF16), pltpu.VMEM((2, n_dp, packed, 128), F32)],
        *got,
        *far,
        flops=FACTOR_FLOPS,
        after=(plane_sum,) if AFTER_PLANE else (),
    )
    piece = add_over(keep + swap(give, 1, 0), far_owner, ())
    for bit in reversed(far_dp):
        near = piece.shape[0] // 2
        piece = piece[:near] + swap(piece[near:], 0, 1 << bit)
    piece = piece.reshape(4, 2 * packed, 128)

    line = call(line_kernel, [((104 + 2 * packed, 128), F32)] * 3, [], total, piece)
    first, first_peer = call(
        first_kernel, [((104 + packed, 128), F32)] * 2, [], total, piece, flops=FIRST_FLOPS, after=line if AFTER_LINE else ()
    )
    line = [swap(line[z - 1], 0, 2 * z) for z in range(1, 4)]
    early = [first, swap(first_peer, 0, 1), swap(first, 2, 0), swap(first_peer, 2, 1)]
    own, peer = call(merge_kernel, [((3 * (104 + packed), 128), F32)] * 2, [], *line)
    late = [own, swap(peer, 0, 1), swap(own, 2, 0), swap(peer, 2, 1)]
    slots = slot_block.shape[1]
    scales = (grad_scale, mean_scale)
    outs = [((16, 32, 288), F32), ((512, 512), F32), ((16, 32, 32), F32), ((half, slots, 288), F32)]
    halves = [((shape[0] // 2, *shape[1:]), kind) for shape, kind in outs]
    scratch = [pltpu.VMEM((640, 128), F32), pltpu.VMEM((48, half // 2, 288), F32)]
    crossed = [swap(jnp.stack(early), 1, 0)] + [swap(v, 1, 0) for v in late]
    mine = call(
        functools.partial(half_kernel, scales), halves, scratch, slot_block, *early, *late, flops=HALF_FLOPS
    )
    group_grad, proj_grad, out_factor, factor_owned = call(
        functools.partial(finish_kernel, scales),
        outs,
        scratch + [pltpu.VMEM(shape, kind) for shape, kind in halves] + [pltpu.SemaphoreType.DMA((8,))],
        slot_block,
        *mine,
        *crossed,
        out_hbm=True,
    )
    return group_grad.transpose(0, 2, 1), proj_grad, out_factor, factor_owned.transpose(1, 0, 2)


def solution(mesh):
    placed = (P(AXES, None, None, None), P(AXES, None, None, None), P(), P(), P(), P(), P())
    return jax.shard_map(
        functools.partial(per_device, mesh.shape["owner"], mesh.shape["dp"]),
        mesh=mesh,
        in_specs=placed,
        out_specs=(P(), P(), P(), P("owner", "dp", None)),
        check_vma=False,
    )
```

```python
import functools
import math

import jax
import jax.numpy as jnp
from jax import lax
from jax.experimental import pallas as pl
from jax.experimental.pallas import tpu as pltpu
from jax.sharding import PartitionSpec as P

AXES = ("owner", "dp")
F32 = jnp.float32
BF16 = jnp.bfloat16
STACK_FLOPS = 4000000000
FACTOR_FLOPS = 4000000000
FIRST_FLOPS = 4000000000
AFTER_CORE = AFTER_PLANE = AFTER_LINE = True
HALF_FLOPS = 1000000000
SEND_FLOPS = 6000000000
LOCAL_FLOPS = 4000000000
VMEM_LIMIT = 48 * 1024 * 1024
PAIRS = ((0, 0), (0, 1), (0, 2), (1, 0), (1, 1), (2, 0), (2, 2))
SAME = {(1, 2): (0, 1), (2, 1): (1, 0)}


def whole_vmem():
    return pl.BlockSpec(memory_space=pltpu.VMEM)


def call(body, outs, scratch, *args, in_hbm=False, out_hbm=False, flops=0, after=()):
    count = len(args)

    def run(*refs):
        body(*refs[:count], *refs[count + len(after) :])

    def place(arg):
        if arg.dtype == jnp.int32:
            return pl.BlockSpec(memory_space=pltpu.SMEM)
        return pl.BlockSpec(memory_space=pltpu.HBM) if in_hbm else whole_vmem()

    return pl.pallas_call(
        run,
        out_shape=[jax.ShapeDtypeStruct(shape, kind) for shape, kind in outs],
        in_specs=[place(a) for a in args] + [pl.BlockSpec(memory_space=pl.ANY) for _ in after],
        out_specs=[pl.BlockSpec(memory_space=pltpu.HBM) if out_hbm else whole_vmem() for _ in outs],
        scratch_shapes=scratch,
        compiler_params=pltpu.CompilerParams(vmem_limit_bytes=VMEM_LIMIT),
        cost_estimate=pl.CostEstimate(flops=flops, bytes_accessed=0, transcendentals=0) if flops else None,
    )(*args, *after)


def plane_id():
    owner, dp = lax.axis_index("owner"), lax.axis_index("dp")
    return (owner & 1) * 4 + ((owner >> 1) & 1) * 2 + (dp & 1)


def cell_id():
    return plane_id() * 4 + ((lax.axis_index("dp") >> 1) & 3)


def shift_rows(value, row_step, col_step):
    images, side, _, width = value.shape
    if col_step != 0:
        flat = value.reshape(images * side, side, width)
        flat = pltpu.roll(flat, (-col_step) % side, 1)
        column = lax.broadcasted_iota(jnp.int32, flat.shape, 1) + col_step
        value = jnp.where((column >= 0) & (column < side), flat, 0.0).reshape(value.shape)
    if row_step != 0:
        edge = jnp.zeros((images, 1, side, width), F32)
        if row_step < 0:
            value = jnp.concatenate([edge, value[:, :-1]], axis=1)
        else:
            value = jnp.concatenate([value[:, 1:], edge], axis=1)
    return value


def send_kernel(x_ref, *refs):
    out_refs, (moved_ref, turned_ref, held) = refs[:4], refs[4:]
    me = cell_id()
    x = x_ref[...].astype(F32)
    x_t = x.reshape(128, 512).T
    turned_ref[...] = x_t.astype(BF16)
    for a in range(3):
        for b in range(3):
            moved_ref[3 * a + b] = shift_rows(x, a - 1, b - 1).reshape(128, 512).astype(BF16)
    for group in range(16):
        held[group ^ (me & 15)] = x_t[32 * group : 32 * group + 32]
    for place, out in enumerate(out_refs):
        out[...] = held[4 * place : 4 * place + 4]


def diagonal(square):
    lane = lax.broadcasted_iota(jnp.int32, (32, 128), 1)
    out = square[96:128]
    for g in (2, 1, 0):
        out = jnp.where(lane < 32 * (g + 1), square[32 * g : 32 * g + 32], out)
    return out


def local_kernel(*refs):
    held, (mine_ref, other_ref), (block_w, hid_t, sums) = refs[:7], refs[7:9], refs[9:]
    moved_ref, turned_ref, og_ref, gw_ref, pw_ref, gain_ref, shift_ref = held
    me = cell_id()
    images = og_ref.shape[0]
    rows = images * 64
    group_at = lax.broadcasted_iota(jnp.int32, (32, 128), 1) // 32
    for q in range(4):
        stacked = gw_ref[4 * q : 4 * q + 4].astype(F32).reshape(128, 288).T
        for s in range(9):
            for g in range(4):
                at = s * 128 + 32 * g
                block_w[q, at : at + 32, :] = jnp.where(group_at == g, stacked[32 * s : 32 * s + 32], 0.0).astype(BF16)
    conv = []
    for q in range(4):
        lhs = jnp.concatenate([moved_ref[s, :, 128 * q : 128 * q + 128] for s in range(9)], axis=1)
        conv.append(jnp.dot(lhs, block_w[q], preferred_element_type=F32))
    conv = jnp.concatenate(conv, axis=1)
    gain = gain_ref[...]
    preact = conv * gain + shift_ref[...]
    hidden = jnp.maximum(preact, 0.0)
    og = og_ref[...].reshape(rows, 512)
    back = lax.dot_general(og, pw_ref[...], (((1,), (1,)), ((), ())), preferred_element_type=F32)
    grad = jnp.where(preact > 0.0, back * gain, 0.0).astype(BF16).astype(F32)
    h_t = hidden.T.astype(BF16)
    for j in range(32):
        hid_t[j ^ me] = h_t[16 * j : 16 * j + 16]
    for half, out in enumerate((mine_ref, other_ref)):
        lhs = hid_t[16 * half : 16 * half + 16].reshape(256, rows)
        part = jnp.dot(lhs, og, preferred_element_type=F32)
        for k in range(16):
            for w in range(4):
                out[k, 16 * w : 16 * w + 16, :] = part[16 * k : 16 * k + 16, 128 * w : 128 * w + 128]
    g_t = grad.reshape(rows, 512).T.astype(BF16)
    grad4 = grad.reshape(images, 8, 8, 512)
    back_moved = [
        shift_rows(grad4, 1 - a, 1 - b).reshape(rows, 512).astype(BF16) for a in range(3) for b in range(3)
    ]
    for q in range(4):
        cut = slice(128 * q, 128 * q + 128)
        rhs = jnp.concatenate([m[:, cut] for m in back_moved], axis=1)
        part = jnp.dot(turned_ref[cut, :], rhs, preferred_element_type=F32)
        for s in range(9):
            at = 320 * q + 32 * s
            sums[at : at + 32, :] = diagonal(part[:, 128 * s : 128 * s + 128])
        part = jnp.dot(g_t[cut], back_moved[4][:, cut], preferred_element_type=F32)
        sums[320 * q + 288 : 320 * q + 320, :] = diagonal(part)
    for half, out in enumerate((mine_ref, other_ref)):
        for k in range(16):
            j = (16 * half + k) ^ me
            out[k, 64:104, :] = sums[pl.ds(pl.multiple_of(40 * j, 8), 40), :]


def packed_rows(count):
    return 5 * count + -(-count // 4)


def factor_kernel(n_dp, *refs):
    parts, (keep_ref, give_ref), (patches, held) = refs[:7], refs[7:9], refs[9:]
    dp, core = lax.axis_index("dp"), lax.axis_index("owner") & 1
    lane = lax.broadcasted_iota(jnp.int32, (32, 128), 1)
    row, col = (lane >> 3) & 7, lane & 7
    sources = [ref[0] for ref in parts[:4]] + [ref[i] for ref in parts[4:] for i in range(4)]
    for src, x_t in enumerate(sources):
        for a in range(3):
            for b in range(3):
                step = (a - 1) * 8 + b - 1
                value = x_t if step == 0 else pltpu.roll(x_t, (-step) % 128, 1)
                keep = (row + a >= 1) & (row + a <= 8) & (col + b >= 1) & (col + b <= 8)
                at = (3 * a + b) * 32
                patches[at : at + 32, 128 * src : 128 * src + 128] = jnp.where(keep, value, 0.0).astype(BF16)
    pieces = []
    for a, width in ((0, 288), (1, 192), (2, 288)):
        part = lax.dot_general(
            patches[96 * a : 96 * a + 96, :],
            patches[:width, :],
            (((1,), (1,)), ((), ())),
            preferred_element_type=F32,
        )
        for pair in PAIRS:
            if pair[0] == a:
                pieces.append(part[:, 96 * pair[1] : 96 * pair[1] + 96])
    full = jnp.concatenate(pieces, axis=1)
    count = 96 // n_dp // 2
    held[...] = jnp.zeros(held.shape, F32)
    for block in range(2 * n_dp):
        at = (block & 1) ^ core, (block >> 1) ^ dp
        rows = full[count * block : count * block + count]
        for tile in range(5):
            held[at[0], at[1], count * tile : count * tile + count, :] = rows[:, 128 * tile : 128 * tile + 128]
        for i in range(count):
            spot = 5 * count + i // 4
            held[at[0], at[1], spot : spot + 1, 32 * (i % 4) : 32 * (i % 4) + 32] = rows[i : i + 1, 640:672]
    keep_ref[...] = held[0]
    give_ref[...] = held[1]


def stack_kernel(*refs):
    for z, out in enumerate(refs[4:]):
        for i, ref in enumerate(refs[:4]):
            out[i] = ref[z + 1]


def copy_kernel(src_ref, out_ref):
    out_ref[...] = src_ref[...]


def line_kernel(total_ref, piece_ref, *line_refs):
    for z, ref in enumerate(line_refs):
        ref[:104, :] = total_ref[...]
        ref[104:, :] = piece_ref[z + 1]


def first_kernel(total_ref, piece_ref, first_ref, peer_ref):
    size = first_ref.shape[0]
    for ref, at in ((first_ref, 0), (peer_ref, size - 104)):
        ref[:104, :] = total_ref[...]
        ref[104:, :] = piece_ref[0, at : at + size - 104, :]


def merge_kernel(*refs):
    parts, (own_ref, peer_ref) = refs[:3], refs[3:]
    size = own_ref.shape[0] // 3
    for z, ref in enumerate(parts):
        at = size * z
        own_ref[at : at + size, :] = ref[:size, :]
        peer_ref[at : at + 104, :] = ref[:104, :]
        peer_ref[at + 104 : at + size, :] = ref[size:, :]


def unpack(scales, slot_ref, parts, outs, sums, blocks):
    group_ref, proj_ref, out_ref, owned_ref = outs
    grad_scale, mean_scale = scales
    me = cell_id() & 15
    count = owned_ref.shape[0]
    step = 104 + packed_rows(count)
    spots = []
    for place in range(4):
        early, late = parts[place], parts[4 + place]
        for z in range(4):
            ref, base = (early, 0) if z == 0 else (late, step * (z - 1))
            spots.append(((4 * place + z) ^ me, ref, base))
    for j, ref, base in spots:
        for w in range(4):
            at = pl.multiple_of(16 * j, 16)
            row = base + 16 * w
            proj_ref[pl.ds(at, 16), 128 * w : 128 * w + 128] = ref[row : row + 16, :] * grad_scale
        sums[pl.ds(pl.multiple_of(40 * j, 8), 40), :] = ref[base + 64 : base + 104, :]
    for q in range(2):
        group_ref[4 * q : 4 * q + 4] = (sums[320 * q : 320 * q + 288, :].T * grad_scale).reshape(4, 32, 288)
        for g in range(4):
            out_ref[4 * q + g] = sums[320 * q + 288 : 320 * q + 320, 32 * g : 32 * g + 32] * mean_scale
    for j, ref, base in spots:
        base += 104
        tiles = [ref[base + count * t : base + count * t + count, :] for t in range(5)]
        last = []
        for i in range(count):
            spot = base + 5 * count + i // 4
            last.append(ref[spot : spot + 1, 32 * (i % 4) : 32 * (i % 4) + 32])
        value = jnp.concatenate(tiles + [jnp.concatenate(last, axis=0)], axis=1) * mean_scale
        for a in range(3):
            pieces = []
            for b in range(3):
                at = 96 * PAIRS.index(SAME.get((a, b), (a, b)))
                pieces.append(value[:, at : at + 96])
            blocks[3 * j + a] = jnp.concatenate(pieces, axis=1)
    owner = lax.axis_index("owner")
    for s in range(owned_ref.shape[1]):
        block = slot_ref[owner, s]
        value = blocks[jnp.maximum(block, 0)]
        owned_ref[:, s, :] = jnp.where(block >= 0, value, 0.0)


def half_kernel(scales, slot_ref, *refs):
    parts, outs, (sums, blocks) = refs[:8], refs[8:12], refs[12:]
    unpack(scales, slot_ref, parts, outs, sums, blocks)


def finish_kernel(scales, slot_ref, *refs):
    mine, (early, *late), outs = refs[:4], refs[4:9], refs[9:13]
    (sums, blocks, *held), sems = refs[13:19], refs[19]
    core = lax.axis_index("owner") & 1

    def send(at, source, which):
        copies = []
        for i, (src, dst) in enumerate(zip(source, outs)):
            size = src.shape[0]
            copies.append(pltpu.make_async_copy(src, dst.at[pl.ds(which * size, size)], sems.at[at + i]))
        return copies

    copies = send(0, mine, core) + send(4, held, 1 - core)
    for copy in copies[:4]:
        copy.start()
    unpack(scales, slot_ref, [early.at[i] for i in range(4)] + late, held, sums, blocks)
    for copy in copies[4:]:
        copy.start()
    for copy in copies:
        copy.wait()


def per_device(n_owner, n_dp, activations, out_grad, group_weight, proj_weight, bn_gain, bn_shift, slot_block):
    def swap(value, owner_mask, dp_mask):
        pairs = [
            (o * n_dp + d, (o ^ owner_mask) * n_dp + (d ^ dp_mask)) for o in range(n_owner) for d in range(n_dp)
        ]
        return lax.ppermute(value, AXES, pairs)

    def add_over(value, owner_bits, dp_bits):
        for bit in owner_bits:
            value = value + swap(value, 1 << bit, 0)
        for bit in dp_bits:
            value = value + swap(value, 0, 1 << bit)
        return value

    far_owner = range(2, n_owner.bit_length() - 1)
    far_dp = range(3, n_dp.bit_length() - 1)
    images = activations.shape[0]
    rows = images * 64
    total_rows = rows * n_owner * n_dp
    grad_scale = 1.0 / math.sqrt(total_rows)
    mean_scale = 1.0 / total_rows

    *sent, moved, turned = call(
        send_kernel,
        [((4, 32, 128), F32)] * 4 + [((9, rows, 512), BF16), ((512, rows), BF16)],
        [pltpu.VMEM((16, 32, 128), F32)],
        activations,
        flops=SEND_FLOPS,
    )
    inputs = [
        moved,
        turned,
        out_grad,
        group_weight.transpose(0, 2, 1),
        proj_weight,
        bn_gain.reshape(1, -1),
        bn_shift.reshape(1, -1),
    ]
    mine, other = call(
        local_kernel,
        [((16, 104, 128), F32)] * 2,
        [
            pltpu.VMEM((4, 1152, 128), BF16),
            pltpu.VMEM((32, 16, rows), BF16),
            pltpu.VMEM((1280, 128), F32),
        ],
        *inputs,
        flops=LOCAL_FLOPS,
    )
    sent, other = lax.optimization_barrier((sent, other))
    got = [sent[0], swap(sent[1], 0, 1), swap(sent[2], 2, 0), swap(sent[3], 2, 1)]
    total = mine + swap(other, 1, 0)
    blocks = call(
        stack_kernel, [((4, 32, 128), F32)] * 3, [], *got, flops=STACK_FLOPS, after=(total,) if AFTER_CORE else ()
    )
    far = [swap(blocks[z - 1], 0, 2 * z) for z in range(1, 4)]
    by_y, by_both, by_x = swap(total[8:12], 2, 0), swap(total[12:16], 2, 1), swap(total[4:8], 0, 1)
    total = total[0:4] + by_y + by_both + by_x
    plane_sum = total
    z2, z3 = swap(total[2], 0, 4), swap(total[3], 0, 6)
    (last,) = call(copy_kernel, [((104, 128), F32)], [], total[1], flops=4000000000, after=(total[2], total[3]))
    z1 = swap(last, 0, 2)
    total = total[0] + z1 + z2 + z3
    total = add_over(total, far_owner, far_dp)
    half = 96 // n_dp
    packed = packed_rows(half // 2)
    keep, give = call(
        functools.partial(factor_kernel, n_dp),
        [((n_dp, packed, 128), F32)] * 2,
        [pltpu.VMEM((288, 2048), BF16), pltpu.VMEM((2, n_dp, packed, 128), F32)],
        *got,
        *far,
        flops=FACTOR_FLOPS,
        after=(plane_sum,) if AFTER_PLANE else (),
    )
    piece = add_over(keep + swap(give, 1, 0), far_owner, ())
    for bit in reversed(far_dp):
        near = piece.shape[0] // 2
        piece = piece[:near] + swap(piece[near:], 0, 1 << bit)
    piece = piece.reshape(4, 2 * packed, 128)

    line = call(line_kernel, [((104 + 2 * packed, 128), F32)] * 3, [], total, piece)
    first, first_peer = call(
        first_kernel, [((104 + packed, 128), F32)] * 2, [], total, piece, flops=FIRST_FLOPS, after=line if AFTER_LINE else ()
    )
    line = [swap(line[z - 1], 0, 2 * z) for z in range(1, 4)]
    early = [first, swap(first_peer, 0, 1), swap(first, 2, 0), swap(first_peer, 2, 1)]
    own, peer = call(merge_kernel, [((3 * (104 + packed), 128), F32)] * 2, [], *line)
    late = [own, swap(peer, 0, 1), swap(own, 2, 0), swap(peer, 2, 1)]
    slots = slot_block.shape[1]
    scales = (grad_scale, mean_scale)
    outs = [((16, 32, 288), F32), ((512, 512), F32), ((16, 32, 32), F32), ((half, slots, 288), F32)]
    halves = [((shape[0] // 2, *shape[1:]), kind) for shape, kind in outs]
    scratch = [pltpu.VMEM((640, 128), F32), pltpu.VMEM((48, half // 2, 288), F32)]
    crossed = [swap(jnp.stack(early), 1, 0)] + [swap(v, 1, 0) for v in late]
    mine = call(
        functools.partial(half_kernel, scales), halves, scratch, slot_block, *early, *late, flops=HALF_FLOPS
    )
    group_grad, proj_grad, out_factor, factor_owned = call(
        functools.partial(finish_kernel, scales),
        outs,
        scratch + [pltpu.VMEM(shape, kind) for shape, kind in halves] + [pltpu.SemaphoreType.DMA((8,))],
        slot_block,
        *mine,
        *crossed,
        out_hbm=True,
    )
    return group_grad.transpose(0, 2, 1), proj_grad, out_factor, factor_owned.transpose(1, 0, 2)


def solution(mesh):
    placed = (P(AXES, None, None, None), P(AXES, None, None, None), P(), P(), P(), P(), P())
    return jax.shard_map(
        functools.partial(per_device, mesh.shape["owner"], mesh.shape["dp"]),
        mesh=mesh,
        in_specs=placed,
        out_specs=(P(), P(), P(), P("owner", "dp", None)),
        check_vma=False,
    )
```

```python
import functools
import math

import jax
import jax.numpy as jnp
from jax import lax
from jax.experimental import pallas as pl
from jax.experimental.pallas import tpu as pltpu
from jax.sharding import PartitionSpec as P

AXES = ("owner", "dp")
F32 = jnp.float32
BF16 = jnp.bfloat16
STACK_FLOPS = 4000000000
FACTOR_FLOPS = 4000000000
FIRST_FLOPS = 4000000000
AFTER_CORE = AFTER_PLANE = AFTER_LINE = True
HALF_FLOPS = 1000000000
SEND_FLOPS = 6000000000
LOCAL_FLOPS = 4000000000
VMEM_LIMIT = 48 * 1024 * 1024
PAIRS = ((0, 0), (0, 1), (0, 2), (1, 0), (1, 1), (2, 0), (2, 2))
SAME = {(1, 2): (0, 1), (2, 1): (1, 0)}


def whole_vmem():
    return pl.BlockSpec(memory_space=pltpu.VMEM)


def call(body, outs, scratch, *args, in_hbm=False, out_hbm=False, flops=0, after=()):
    count = len(args)

    def run(*refs):
        body(*refs[:count], *refs[count + len(after) :])

    def place(arg):
        if arg.dtype == jnp.int32:
            return pl.BlockSpec(memory_space=pltpu.SMEM)
        return pl.BlockSpec(memory_space=pltpu.HBM) if in_hbm else whole_vmem()

    return pl.pallas_call(
        run,
        out_shape=[jax.ShapeDtypeStruct(shape, kind) for shape, kind in outs],
        in_specs=[place(a) for a in args] + [pl.BlockSpec(memory_space=pl.ANY) for _ in after],
        out_specs=[pl.BlockSpec(memory_space=pltpu.HBM) if out_hbm else whole_vmem() for _ in outs],
        scratch_shapes=scratch,
        compiler_params=pltpu.CompilerParams(vmem_limit_bytes=VMEM_LIMIT),
        cost_estimate=pl.CostEstimate(flops=flops, bytes_accessed=0, transcendentals=0) if flops else None,
    )(*args, *after)


def plane_id():
    owner, dp = lax.axis_index("owner"), lax.axis_index("dp")
    return (owner & 1) * 4 + ((owner >> 1) & 1) * 2 + (dp & 1)


def cell_id():
    return plane_id() * 4 + ((lax.axis_index("dp") >> 1) & 3)


def send_kernel(x_ref, *refs):
    out_refs, held = refs[:4], refs[4]
    me = cell_id()
    x_t = x_ref[...].astype(F32).reshape(128, 512).T
    for group in range(16):
        held[group ^ (me & 15)] = x_t[32 * group : 32 * group + 32]
    for place, out in enumerate(out_refs):
        out[...] = held[4 * place : 4 * place + 4]


def shift_rows(value, row_step, col_step):
    images, side, _, width = value.shape
    if col_step != 0:
        flat = value.reshape(images * side, side, width)
        flat = pltpu.roll(flat, (-col_step) % side, 1)
        column = lax.broadcasted_iota(jnp.int32, flat.shape, 1) + col_step
        value = jnp.where((column >= 0) & (column < side), flat, 0.0).reshape(value.shape)
    if row_step != 0:
        edge = jnp.zeros((images, 1, side, width), F32)
        if row_step < 0:
            value = jnp.concatenate([edge, value[:, :-1]], axis=1)
        else:
            value = jnp.concatenate([value[:, 1:], edge], axis=1)
    return value


def diagonal(square):
    lane = lax.broadcasted_iota(jnp.int32, (32, 128), 1)
    out = square[96:128]
    for g in (2, 1, 0):
        out = jnp.where(lane < 32 * (g + 1), square[32 * g : 32 * g + 32], out)
    return out


def local_kernel(*refs):
    held, (mine_ref, other_ref), (block_w, hid_t, sums) = refs[:6], refs[6:8], refs[8:]
    x_ref, og_ref, gw_ref, pw_ref, gain_ref, shift_ref = held
    me = cell_id()
    images = x_ref.shape[0]
    rows = images * 64
    group_at = lax.broadcasted_iota(jnp.int32, (32, 128), 1) // 32
    for q in range(4):
        stacked = gw_ref[4 * q : 4 * q + 4].astype(F32).reshape(128, 288).T
        for s in range(9):
            for g in range(4):
                at = s * 128 + 32 * g
                block_w[q, at : at + 32, :] = jnp.where(group_at == g, stacked[32 * s : 32 * s + 32], 0.0).astype(BF16)
    x = x_ref[...].astype(F32)
    moved = [
        shift_rows(x, a - 1, b - 1).reshape(rows, 512).astype(BF16) for a in range(3) for b in range(3)
    ]
    conv = []
    for q in range(4):
        lhs = jnp.concatenate([m[:, 128 * q : 128 * q + 128] for m in moved], axis=1)
        conv.append(jnp.dot(lhs, block_w[q], preferred_element_type=F32))
    conv = jnp.concatenate(conv, axis=1)
    gain = gain_ref[...]
    preact = conv * gain + shift_ref[...]
    hidden = jnp.maximum(preact, 0.0)
    og = og_ref[...].reshape(rows, 512)
    back = lax.dot_general(og, pw_ref[...], (((1,), (1,)), ((), ())), preferred_element_type=F32)
    grad = jnp.where(preact > 0.0, back * gain, 0.0).astype(BF16).astype(F32)
    h_t = hidden.T.astype(BF16)
    for j in range(32):
        hid_t[j ^ me] = h_t[16 * j : 16 * j + 16]
    for half, out in enumerate((mine_ref, other_ref)):
        lhs = hid_t[16 * half : 16 * half + 16].reshape(256, rows)
        part = jnp.dot(lhs, og, preferred_element_type=F32)
        for k in range(16):
            for w in range(4):
                out[k, 16 * w : 16 * w + 16, :] = part[16 * k : 16 * k + 16, 128 * w : 128 * w + 128]
    x_t = x.reshape(rows, 512).T.astype(BF16)
    g_t = grad.reshape(rows, 512).T.astype(BF16)
    grad4 = grad.reshape(images, 8, 8, 512)
    back_moved = [
        shift_rows(grad4, 1 - a, 1 - b).reshape(rows, 512).astype(BF16) for a in range(3) for b in range(3)
    ]
    for q in range(4):
        cut = slice(128 * q, 128 * q + 128)
        rhs = jnp.concatenate([m[:, cut] for m in back_moved], axis=1)
        part = jnp.dot(x_t[cut], rhs, preferred_element_type=F32)
        for s in range(9):
            at = 320 * q + 32 * s
            sums[at : at + 32, :] = diagonal(part[:, 128 * s : 128 * s + 128])
        part = jnp.dot(g_t[cut], back_moved[4][:, cut], preferred_element_type=F32)
        sums[320 * q + 288 : 320 * q + 320, :] = diagonal(part)
    for half, out in enumerate((mine_ref, other_ref)):
        for k in range(16):
            j = (16 * half + k) ^ me
            out[k, 64:104, :] = sums[pl.ds(pl.multiple_of(40 * j, 8), 40), :]


def packed_rows(count):
    return 5 * count + -(-count // 4)


def factor_kernel(n_dp, *refs):
    parts, (keep_ref, give_ref), (patches, held) = refs[:7], refs[7:9], refs[9:]
    dp, core = lax.axis_index("dp"), lax.axis_index("owner") & 1
    lane = lax.broadcasted_iota(jnp.int32, (32, 128), 1)
    row, col = (lane >> 3) & 7, lane & 7
    sources = [ref[0] for ref in parts[:4]] + [ref[i] for ref in parts[4:] for i in range(4)]
    for src, x_t in enumerate(sources):
        for a in range(3):
            for b in range(3):
                step = (a - 1) * 8 + b - 1
                value = x_t if step == 0 else pltpu.roll(x_t, (-step) % 128, 1)
                keep = (row + a >= 1) & (row + a <= 8) & (col + b >= 1) & (col + b <= 8)
                at = (3 * a + b) * 32
                patches[at : at + 32, 128 * src : 128 * src + 128] = jnp.where(keep, value, 0.0).astype(BF16)
    pieces = []
    for a, width in ((0, 288), (1, 192), (2, 288)):
        part = lax.dot_general(
            patches[96 * a : 96 * a + 96, :],
            patches[:width, :],
            (((1,), (1,)), ((), ())),
            preferred_element_type=F32,
        )
        for pair in PAIRS:
            if pair[0] == a:
                pieces.append(part[:, 96 * pair[1] : 96 * pair[1] + 96])
    full = jnp.concatenate(pieces, axis=1)
    count = 96 // n_dp // 2
    held[...] = jnp.zeros(held.shape, F32)
    for block in range(2 * n_dp):
        at = (block & 1) ^ core, (block >> 1) ^ dp
        rows = full[count * block : count * block + count]
        for tile in range(5):
            held[at[0], at[1], count * tile : count * tile + count, :] = rows[:, 128 * tile : 128 * tile + 128]
        for i in range(count):
            spot = 5 * count + i // 4
            held[at[0], at[1], spot : spot + 1, 32 * (i % 4) : 32 * (i % 4) + 32] = rows[i : i + 1, 640:672]
    keep_ref[...] = held[0]
    give_ref[...] = held[1]


def stack_kernel(*refs):
    for z, out in enumerate(refs[4:]):
        for i, ref in enumerate(refs[:4]):
            out[i] = ref[z + 1]


def copy_kernel(src_ref, out_ref):
    out_ref[...] = src_ref[...]


def line_kernel(total_ref, piece_ref, *line_refs):
    for z, ref in enumerate(line_refs):
        ref[:104, :] = total_ref[...]
        ref[104:, :] = piece_ref[z + 1]


def first_kernel(total_ref, piece_ref, first_ref, peer_ref):
    size = first_ref.shape[0]
    for ref, at in ((first_ref, 0), (peer_ref, size - 104)):
        ref[:104, :] = total_ref[...]
        ref[104:, :] = piece_ref[0, at : at + size - 104, :]


def merge_kernel(*refs):
    parts, (own_ref, peer_ref) = refs[:3], refs[3:]
    size = own_ref.shape[0] // 3
    for z, ref in enumerate(parts):
        at = size * z
        own_ref[at : at + size, :] = ref[:size, :]
        peer_ref[at : at + 104, :] = ref[:104, :]
        peer_ref[at + 104 : at + size, :] = ref[size:, :]


def unpack(scales, slot_ref, parts, outs, sums, blocks, ready=lambda which: None):
    group_ref, proj_ref, out_ref, owned_ref = outs
    grad_scale, mean_scale = scales
    me = cell_id() & 15
    count = owned_ref.shape[0]
    step = 104 + packed_rows(count)
    spots = []
    for place in range(4):
        early, late = parts[place], parts[4 + place]
        for z in range(4):
            ref, base = (early, 0) if z == 0 else (late, step * (z - 1))
            spots.append(((4 * place + z) ^ me, ref, base))
    for j, ref, base in spots:
        for w in range(4):
            at = pl.multiple_of(16 * j, 16)
            row = base + 16 * w
            proj_ref[pl.ds(at, 16), 128 * w : 128 * w + 128] = ref[row : row + 16, :] * grad_scale
        sums[pl.ds(pl.multiple_of(40 * j, 8), 40), :] = ref[base + 64 : base + 104, :]
    ready(1)
    for q in range(2):
        group_ref[4 * q : 4 * q + 4] = (sums[320 * q : 320 * q + 288, :].T * grad_scale).reshape(4, 32, 288)
        for g in range(4):
            out_ref[4 * q + g] = sums[320 * q + 288 : 320 * q + 320, 32 * g : 32 * g + 32] * mean_scale
    ready(0)
    ready(2)
    for j, ref, base in spots:
        base += 104
        tiles = [ref[base + count * t : base + count * t + count, :] for t in range(5)]
        last = []
        for i in range(count):
            spot = base + 5 * count + i // 4
            last.append(ref[spot : spot + 1, 32 * (i % 4) : 32 * (i % 4) + 32])
        value = jnp.concatenate(tiles + [jnp.concatenate(last, axis=0)], axis=1) * mean_scale
        for a in range(3):
            pieces = []
            for b in range(3):
                at = 96 * PAIRS.index(SAME.get((a, b), (a, b)))
                pieces.append(value[:, at : at + 96])
            blocks[3 * j + a] = jnp.concatenate(pieces, axis=1)
    owner = lax.axis_index("owner")
    for s in range(owned_ref.shape[1]):
        block = slot_ref[owner, s]
        value = blocks[jnp.maximum(block, 0)]
        owned_ref[:, s, :] = jnp.where(block >= 0, value, 0.0)
    ready(3)


def half_kernel(scales, slot_ref, *refs):
    parts, outs, (sums, blocks) = refs[:8], refs[8:12], refs[12:]
    unpack(scales, slot_ref, parts, outs, sums, blocks)


def finish_kernel(scales, slot_ref, *refs):
    mine, (early, *late), outs = refs[:4], refs[4:9], refs[9:13]
    (sums, blocks, *held), sems = refs[13:19], refs[19]
    core = lax.axis_index("owner") & 1

    def send(at, source, which):
        copies = []
        for i, (src, dst) in enumerate(zip(source, outs)):
            size = src.shape[0]
            copies.append(pltpu.make_async_copy(src, dst.at[pl.ds(which * size, size)], sems.at[at + i]))
        return copies

    copies = send(0, mine, core) + send(4, held, 1 - core)
    for copy in copies[:4]:
        copy.start()
    unpack(scales, slot_ref, [early.at[i] for i in range(4)] + late, held, sums, blocks, lambda which: copies[4 + which].start())
    for copy in copies:
        copy.wait()


def per_device(n_owner, n_dp, activations, out_grad, group_weight, proj_weight, bn_gain, bn_shift, slot_block):
    def swap(value, owner_mask, dp_mask):
        pairs = [
            (o * n_dp + d, (o ^ owner_mask) * n_dp + (d ^ dp_mask)) for o in range(n_owner) for d in range(n_dp)
        ]
        return lax.ppermute(value, AXES, pairs)

    def add_over(value, owner_bits, dp_bits):
        for bit in owner_bits:
            value = value + swap(value, 1 << bit, 0)
        for bit in dp_bits:
            value = value + swap(value, 0, 1 << bit)
        return value

    far_owner = range(2, n_owner.bit_length() - 1)
    far_dp = range(3, n_dp.bit_length() - 1)
    images = activations.shape[0]
    rows = images * 64
    total_rows = rows * n_owner * n_dp
    grad_scale = 1.0 / math.sqrt(total_rows)
    mean_scale = 1.0 / total_rows

    sent = call(
        send_kernel,
        [((4, 32, 128), F32)] * 4,
        [pltpu.VMEM((16, 32, 128), F32)],
        activations,
        flops=SEND_FLOPS,
    )
    inputs = [
        activations,
        out_grad,
        group_weight.transpose(0, 2, 1),
        proj_weight,
        bn_gain.reshape(1, -1),
        bn_shift.reshape(1, -1),
    ]
    mine, other = call(
        local_kernel,
        [((16, 104, 128), F32)] * 2,
        [
            pltpu.VMEM((4, 1152, 128), BF16),
            pltpu.VMEM((32, 16, rows), BF16),
            pltpu.VMEM((1280, 128), F32),
        ],
        *inputs,
        flops=LOCAL_FLOPS,
    )
    sent, other = lax.optimization_barrier((sent, other))
    got = [sent[0], swap(sent[1], 0, 1), swap(sent[2], 2, 0), swap(sent[3], 2, 1)]
    total = mine + swap(other, 1, 0)
    blocks = call(
        stack_kernel, [((4, 32, 128), F32)] * 3, [], *got, flops=STACK_FLOPS, after=(total,) if AFTER_CORE else ()
    )
    far = [swap(blocks[z - 1], 0, 2 * z) for z in range(1, 4)]
    by_y, by_both, by_x = swap(total[8:12], 2, 0), swap(total[12:16], 2, 1), swap(total[4:8], 0, 1)
    total = total[0:4] + by_y + by_both + by_x
    plane_sum = total
    z2, z3 = swap(total[2], 0, 4), swap(total[3], 0, 6)
    (last,) = call(copy_kernel, [((104, 128), F32)], [], total[1], flops=4000000000, after=(total[2], total[3]))
    z1 = swap(last, 0, 2)
    total = total[0] + z1 + z2 + z3
    total = add_over(total, far_owner, far_dp)
    half = 96 // n_dp
    packed = packed_rows(half // 2)
    keep, give = call(
        functools.partial(factor_kernel, n_dp),
        [((n_dp, packed, 128), F32)] * 2,
        [pltpu.VMEM((288, 2048), BF16), pltpu.VMEM((2, n_dp, packed, 128), F32)],
        *got,
        *far,
        flops=FACTOR_FLOPS,
        after=(plane_sum,) if AFTER_PLANE else (),
    )
    piece = add_over(keep + swap(give, 1, 0), far_owner, ())
    for bit in reversed(far_dp):
        near = piece.shape[0] // 2
        piece = piece[:near] + swap(piece[near:], 0, 1 << bit)
    piece = piece.reshape(4, 2 * packed, 128)

    line = call(line_kernel, [((104 + 2 * packed, 128), F32)] * 3, [], total, piece)
    first, first_peer = call(
        first_kernel, [((104 + packed, 128), F32)] * 2, [], total, piece, flops=FIRST_FLOPS, after=line if AFTER_LINE else ()
    )
    line = [swap(line[z - 1], 0, 2 * z) for z in range(1, 4)]
    early = [first, swap(first_peer, 0, 1), swap(first, 2, 0), swap(first_peer, 2, 1)]
    own, peer = call(merge_kernel, [((3 * (104 + packed), 128), F32)] * 2, [], *line)
    late = [own, swap(peer, 0, 1), swap(own, 2, 0), swap(peer, 2, 1)]
    slots = slot_block.shape[1]
    scales = (grad_scale, mean_scale)
    outs = [((16, 32, 288), F32), ((512, 512), F32), ((16, 32, 32), F32), ((half, slots, 288), F32)]
    halves = [((shape[0] // 2, *shape[1:]), kind) for shape, kind in outs]
    scratch = [pltpu.VMEM((640, 128), F32), pltpu.VMEM((48, half // 2, 288), F32)]
    crossed = [swap(jnp.stack(early), 1, 0)] + [swap(v, 1, 0) for v in late]
    mine = call(
        functools.partial(half_kernel, scales), halves, scratch, slot_block, *early, *late, flops=HALF_FLOPS
    )
    group_grad, proj_grad, out_factor, factor_owned = call(
        functools.partial(finish_kernel, scales),
        outs,
        scratch + [pltpu.VMEM(shape, kind) for shape, kind in halves] + [pltpu.SemaphoreType.DMA((8,))],
        slot_block,
        *mine,
        *crossed,
        out_hbm=True,
    )
    return group_grad.transpose(0, 2, 1), proj_grad, out_factor, factor_owned.transpose(1, 0, 2)


def solution(mesh):
    placed = (P(AXES, None, None, None), P(AXES, None, None, None), P(), P(), P(), P(), P())
    return jax.shard_map(
        functools.partial(per_device, mesh.shape["owner"], mesh.shape["dp"]),
        mesh=mesh,
        in_specs=placed,
        out_specs=(P(), P(), P(), P("owner", "dp", None)),
        check_vma=False,
    )
```

```python
import functools
import math

import jax
import jax.numpy as jnp
from jax import lax
from jax.experimental import pallas as pl
from jax.experimental.pallas import tpu as pltpu
from jax.sharding import PartitionSpec as P

AXES = ("owner", "dp")
F32 = jnp.float32
BF16 = jnp.bfloat16
STACK_FLOPS = 4000000000
FACTOR_FLOPS = 4000000000
FIRST_FLOPS = 4000000000
AFTER_CORE = AFTER_PLANE = AFTER_LINE = True
HALF_FLOPS = 1000000000
SEND_FLOPS = 6000000000
LOCAL_FLOPS = 4000000000
VMEM_LIMIT = 48 * 1024 * 1024
PAIRS = ((0, 0), (0, 1), (0, 2), (1, 0), (1, 1), (2, 0), (2, 2))
SAME = {(1, 2): (0, 1), (2, 1): (1, 0)}


def whole_vmem():
    return pl.BlockSpec(memory_space=pltpu.VMEM)


def call(body, outs, scratch, *args, in_hbm=False, out_hbm=False, flops=0, after=()):
    count = len(args)

    def run(*refs):
        body(*refs[:count], *refs[count + len(after) :])

    def place(arg):
        if arg.dtype == jnp.int32:
            return pl.BlockSpec(memory_space=pltpu.SMEM)
        return pl.BlockSpec(memory_space=pltpu.HBM) if in_hbm else whole_vmem()

    return pl.pallas_call(
        run,
        out_shape=[jax.ShapeDtypeStruct(shape, kind) for shape, kind in outs],
        in_specs=[place(a) for a in args] + [pl.BlockSpec(memory_space=pl.ANY) for _ in after],
        out_specs=[pl.BlockSpec(memory_space=pltpu.HBM) if out_hbm else whole_vmem() for _ in outs],
        scratch_shapes=scratch,
        compiler_params=pltpu.CompilerParams(vmem_limit_bytes=VMEM_LIMIT),
        cost_estimate=pl.CostEstimate(flops=flops, bytes_accessed=0, transcendentals=0) if flops else None,
    )(*args, *after)


def plane_id():
    owner, dp = lax.axis_index("owner"), lax.axis_index("dp")
    return (owner & 1) * 4 + ((owner >> 1) & 1) * 2 + (dp & 1)


def cell_id():
    return plane_id() * 4 + ((lax.axis_index("dp") >> 1) & 3)


def send_kernel(x_ref, *refs):
    out_refs, held = refs[:4], refs[4]
    me = cell_id()
    x_t = x_ref[...].astype(F32).reshape(128, 512).T
    for group in range(16):
        held[group ^ (me & 15)] = x_t[32 * group : 32 * group + 32]
    for place, out in enumerate(out_refs):
        out[...] = held[4 * place : 4 * place + 4]


def shift_rows(value, row_step, col_step):
    images, side, _, width = value.shape
    if col_step != 0:
        flat = value.reshape(images * side, side, width)
        flat = pltpu.roll(flat, (-col_step) % side, 1)
        column = lax.broadcasted_iota(jnp.int32, flat.shape, 1) + col_step
        value = jnp.where((column >= 0) & (column < side), flat, 0.0).reshape(value.shape)
    if row_step != 0:
        edge = jnp.zeros((images, 1, side, width), F32)
        if row_step < 0:
            value = jnp.concatenate([edge, value[:, :-1]], axis=1)
        else:
            value = jnp.concatenate([value[:, 1:], edge], axis=1)
    return value


def diagonal(square):
    lane = lax.broadcasted_iota(jnp.int32, (32, 128), 1)
    out = square[96:128]
    for g in (2, 1, 0):
        out = jnp.where(lane < 32 * (g + 1), square[32 * g : 32 * g + 32], out)
    return out


def local_kernel(*refs):
    held, (mine_ref, other_ref), (block_w, hid_t, sums) = refs[:6], refs[6:8], refs[8:]
    x_ref, og_ref, gw_ref, pw_ref, gain_ref, shift_ref = held
    me = cell_id()
    images = x_ref.shape[0]
    rows = images * 64
    group_at = lax.broadcasted_iota(jnp.int32, (32, 128), 1) // 32
    for q in range(4):
        stacked = gw_ref[4 * q : 4 * q + 4].astype(F32).reshape(128, 288).T
        for s in range(9):
            for g in range(4):
                at = s * 128 + 32 * g
                block_w[q, at : at + 32, :] = jnp.where(group_at == g, stacked[32 * s : 32 * s + 32], 0.0).astype(BF16)
    x = x_ref[...].astype(F32)
    moved = [
        shift_rows(x, a - 1, b - 1).reshape(rows, 512).astype(BF16) for a in range(3) for b in range(3)
    ]
    conv = []
    for q in range(4):
        lhs = jnp.concatenate([m[:, 128 * q : 128 * q + 128] for m in moved], axis=1)
        conv.append(jnp.dot(lhs, block_w[q], preferred_element_type=F32))
    conv = jnp.concatenate(conv, axis=1)
    gain = gain_ref[...]
    preact = conv * gain + shift_ref[...]
    hidden = jnp.maximum(preact, 0.0)
    og = og_ref[...].reshape(rows, 512)
    back = lax.dot_general(og, pw_ref[...], (((1,), (1,)), ((), ())), preferred_element_type=F32)
    grad = jnp.where(preact > 0.0, back * gain, 0.0).astype(BF16).astype(F32)
    h_t = hidden.T.astype(BF16)
    for j in range(32):
        hid_t[j ^ me] = h_t[16 * j : 16 * j + 16]
    for half, out in enumerate((mine_ref, other_ref)):
        lhs = hid_t[16 * half : 16 * half + 16].reshape(256, rows)
        part = jnp.dot(lhs, og, preferred_element_type=F32)
        for k in range(16):
            for w in range(4):
                out[k, 16 * w : 16 * w + 16, :] = part[16 * k : 16 * k + 16, 128 * w : 128 * w + 128]
    x_t = x.reshape(rows, 512).T.astype(BF16)
    g_t = grad.reshape(rows, 512).T.astype(BF16)
    grad4 = grad.reshape(images, 8, 8, 512)
    back_moved = [
        shift_rows(grad4, 1 - a, 1 - b).reshape(rows, 512).astype(BF16) for a in range(3) for b in range(3)
    ]
    for q in range(4):
        cut = slice(128 * q, 128 * q + 128)
        rhs = jnp.concatenate([m[:, cut] for m in back_moved], axis=1)
        part = jnp.dot(x_t[cut], rhs, preferred_element_type=F32)
        for s in range(9):
            at = 320 * q + 32 * s
            sums[at : at + 32, :] = diagonal(part[:, 128 * s : 128 * s + 128])
        part = jnp.dot(g_t[cut], back_moved[4][:, cut], preferred_element_type=F32)
        sums[320 * q + 288 : 320 * q + 320, :] = diagonal(part)
    for half, out in enumerate((mine_ref, other_ref)):
        for k in range(16):
            j = (16 * half + k) ^ me
            out[k, 64:104, :] = sums[pl.ds(pl.multiple_of(40 * j, 8), 40), :]


def packed_rows(count):
    return 5 * count + -(-count // 4)


def factor_kernel(n_dp, *refs):
    parts, (keep_ref, give_ref), (patches, held) = refs[:7], refs[7:9], refs[9:]
    dp, core = lax.axis_index("dp"), lax.axis_index("owner") & 1
    lane = lax.broadcasted_iota(jnp.int32, (32, 128), 1)
    row, col = (lane >> 3) & 7, lane & 7
    sources = [ref[0] for ref in parts[:4]] + [ref[i] for ref in parts[4:] for i in range(4)]
    for src, x_t in enumerate(sources):
        for a in range(3):
            for b in range(3):
                step = (a - 1) * 8 + b - 1
                value = x_t if step == 0 else pltpu.roll(x_t, (-step) % 128, 1)
                keep = (row + a >= 1) & (row + a <= 8) & (col + b >= 1) & (col + b <= 8)
                at = (3 * a + b) * 32
                patches[at : at + 32, 128 * src : 128 * src + 128] = jnp.where(keep, value, 0.0).astype(BF16)
    pieces = []
    for a, width in ((0, 288), (1, 192), (2, 288)):
        part = lax.dot_general(
            patches[96 * a : 96 * a + 96, :],
            patches[:width, :],
            (((1,), (1,)), ((), ())),
            preferred_element_type=F32,
        )
        for pair in PAIRS:
            if pair[0] == a:
                pieces.append(part[:, 96 * pair[1] : 96 * pair[1] + 96])
    full = jnp.concatenate(pieces, axis=1)
    count = 96 // n_dp // 2
    held[...] = jnp.zeros(held.shape, F32)
    for block in range(2 * n_dp):
        at = (block & 1) ^ core, (block >> 1) ^ dp
        rows = full[count * block : count * block + count]
        for tile in range(5):
            held[at[0], at[1], count * tile : count * tile + count, :] = rows[:, 128 * tile : 128 * tile + 128]
        for i in range(count):
            spot = 5 * count + i // 4
            held[at[0], at[1], spot : spot + 1, 32 * (i % 4) : 32 * (i % 4) + 32] = rows[i : i + 1, 640:672]
    keep_ref[...] = held[0]
    give_ref[...] = held[1]


def stack_kernel(*refs):
    for z, out in enumerate(refs[4:]):
        for i, ref in enumerate(refs[:4]):
            out[i] = ref[z + 1]


def copy_kernel(src_ref, out_ref):
    out_ref[...] = src_ref[...]


def line_kernel(total_ref, piece_ref, *line_refs):
    for z, ref in enumerate(line_refs):
        ref[:104, :] = total_ref[...]
        ref[104:, :] = piece_ref[z + 1]


def first_kernel(total_ref, piece_ref, first_ref, peer_ref):
    size = first_ref.shape[0]
    for ref, at in ((first_ref, 0), (peer_ref, size - 104)):
        ref[:104, :] = total_ref[...]
        ref[104:, :] = piece_ref[0, at : at + size - 104, :]


def merge_kernel(*refs):
    parts, (own_ref, peer_ref) = refs[:3], refs[3:]
    size = own_ref.shape[0] // 3
    for z, ref in enumerate(parts):
        at = size * z
        own_ref[at : at + size, :] = ref[:size, :]
        peer_ref[at : at + 104, :] = ref[:104, :]
        peer_ref[at + 104 : at + size, :] = ref[size:, :]


def unpack(scales, slot_ref, parts, outs, sums, blocks, ready=lambda which: None):
    group_ref, proj_ref, out_ref, owned_ref = outs
    grad_scale, mean_scale = scales
    me = cell_id() & 15
    count = owned_ref.shape[0]
    step = 104 + packed_rows(count)
    spots = []
    for place in range(4):
        early, late = parts[place], parts[4 + place]
        for z in range(4):
            ref, base = (early, 0) if z == 0 else (late, step * (z - 1))
            spots.append(((4 * place + z) ^ me, ref, base))
    for j, ref, base in spots:
        for w in range(4):
            at = pl.multiple_of(16 * j, 16)
            row = base + 16 * w
            proj_ref[pl.ds(at, 16), 128 * w : 128 * w + 128] = ref[row : row + 16, :] * grad_scale
        sums[pl.ds(pl.multiple_of(40 * j, 8), 40), :] = ref[base + 64 : base + 104, :]
    ready(1)
    for q in range(2):
        group_ref[4 * q : 4 * q + 4] = (sums[320 * q : 320 * q + 288, :].T * grad_scale).reshape(4, 32, 288)
        for g in range(4):
            out_ref[4 * q + g] = sums[320 * q + 288 : 320 * q + 320, 32 * g : 32 * g + 32] * mean_scale
    ready(0)
    ready(2)
    for j, ref, base in spots:
        base += 104
        tiles = [ref[base + count * t : base + count * t + count, :] for t in range(5)]
        last = []
        for i in range(count):
            spot = base + 5 * count + i // 4
            last.append(ref[spot : spot + 1, 32 * (i % 4) : 32 * (i % 4) + 32])
        value = jnp.concatenate(tiles + [jnp.concatenate(last, axis=0)], axis=1) * mean_scale
        for a in range(3):
            pieces = []
            for b in range(3):
                at = 96 * PAIRS.index(SAME.get((a, b), (a, b)))
                pieces.append(value[:, at : at + 96])
            blocks[3 * j + a] = jnp.concatenate(pieces, axis=1)
    owner = lax.axis_index("owner")
    for s in range(owned_ref.shape[1]):
        block = slot_ref[owner, s]
        value = blocks[jnp.maximum(block, 0)]
        owned_ref[:, s, :] = jnp.where(block >= 0, value, 0.0)
    ready(3)


def half_kernel(scales, slot_ref, *refs):
    parts, outs, (sums, blocks) = refs[:8], refs[8:12], refs[12:]
    unpack(scales, slot_ref, parts, outs, sums, blocks)


def finish_kernel(scales, slot_ref, *refs):
    mine, (early, *late), outs = refs[:4], refs[4:9], refs[9:13]
    (sums, blocks, *held), sems = refs[13:19], refs[19]
    core = lax.axis_index("owner") & 1

    def send(at, source, which):
        copies = []
        for i, (src, dst) in enumerate(zip(source, outs)):
            size = src.shape[0]
            copies.append(pltpu.make_async_copy(src, dst.at[pl.ds(which * size, size)], sems.at[at + i]))
        return copies

    copies = send(0, mine, core) + send(4, held, 1 - core)
    for copy in copies[:4]:
        copy.start()
    unpack(scales, slot_ref, [early.at[i] for i in range(4)] + late, held, sums, blocks, lambda which: copies[4 + which].start())
    for copy in copies:
        copy.wait()


def per_device(n_owner, n_dp, activations, out_grad, group_weight, proj_weight, bn_gain, bn_shift, slot_block):
    def swap(value, owner_mask, dp_mask):
        pairs = [
            (o * n_dp + d, (o ^ owner_mask) * n_dp + (d ^ dp_mask)) for o in range(n_owner) for d in range(n_dp)
        ]
        return lax.ppermute(value, AXES, pairs)

    def add_over(value, owner_bits, dp_bits):
        for bit in owner_bits:
            value = value + swap(value, 1 << bit, 0)
        for bit in dp_bits:
            value = value + swap(value, 0, 1 << bit)
        return value

    far_owner = range(2, n_owner.bit_length() - 1)
    far_dp = range(3, n_dp.bit_length() - 1)
    images = activations.shape[0]
    rows = images * 64
    total_rows = rows * n_owner * n_dp
    grad_scale = 1.0 / math.sqrt(total_rows)
    mean_scale = 1.0 / total_rows

    sent = call(
        send_kernel,
        [((4, 32, 128), F32)] * 4,
        [pltpu.VMEM((16, 32, 128), F32)],
        activations,
        flops=SEND_FLOPS,
    )
    inputs = [
        activations,
        out_grad,
        group_weight.transpose(0, 2, 1),
        proj_weight,
        bn_gain.reshape(1, -1),
        bn_shift.reshape(1, -1),
    ]
    mine, other = call(
        local_kernel,
        [((16, 104, 128), F32)] * 2,
        [
            pltpu.VMEM((4, 1152, 128), BF16),
            pltpu.VMEM((32, 16, rows), BF16),
            pltpu.VMEM((1280, 128), F32),
        ],
        *inputs,
        flops=LOCAL_FLOPS,
    )
    sent, other = lax.optimization_barrier((sent, other))
    got = [sent[0], swap(sent[1], 0, 1), swap(sent[2], 2, 0), swap(sent[3], 2, 1)]
    total = mine + swap(other, 1, 0)
    blocks = call(
        stack_kernel, [((4, 32, 128), F32)] * 3, [], *got, flops=STACK_FLOPS, after=(total,) if AFTER_CORE else ()
    )
    far = [swap(blocks[z - 1], 0, 2 * z) for z in (3, 2, 1)][::-1]
    by_x, by_both, by_y = swap(total[4:8], 0, 1), swap(total[12:16], 2, 1), swap(total[8:12], 2, 0)
    total = total[0:4] + by_y + by_both + by_x
    plane_sum = total
    z2, z3 = swap(total[2], 0, 4), swap(total[3], 0, 6)
    (last,) = call(copy_kernel, [((104, 128), F32)], [], total[1], flops=4000000000, after=(total[2], total[3]))
    z1 = swap(last, 0, 2)
    total = total[0] + z1 + z2 + z3
    total = add_over(total, far_owner, far_dp)
    half = 96 // n_dp
    packed = packed_rows(half // 2)
    keep, give = call(
        functools.partial(factor_kernel, n_dp),
        [((n_dp, packed, 128), F32)] * 2,
        [pltpu.VMEM((288, 2048), BF16), pltpu.VMEM((2, n_dp, packed, 128), F32)],
        *got,
        *far,
        flops=FACTOR_FLOPS,
        after=(plane_sum,) if AFTER_PLANE else (),
    )
    piece = add_over(keep + swap(give, 1, 0), far_owner, ())
    for bit in reversed(far_dp):
        near = piece.shape[0] // 2
        piece = piece[:near] + swap(piece[near:], 0, 1 << bit)
    piece = piece.reshape(4, 2 * packed, 128)

    line = call(line_kernel, [((104 + 2 * packed, 128), F32)] * 3, [], total, piece)
    first, first_peer = call(
        first_kernel, [((104 + packed, 128), F32)] * 2, [], total, piece, flops=FIRST_FLOPS, after=line if AFTER_LINE else ()
    )
    line = [swap(line[z - 1], 0, 2 * z) for z in range(1, 4)]
    early = [first, swap(first_peer, 0, 1), swap(first, 2, 0), swap(first_peer, 2, 1)]
    own, peer = call(merge_kernel, [((3 * (104 + packed), 128), F32)] * 2, [], *line)
    late = [own, swap(peer, 0, 1), swap(own, 2, 0), swap(peer, 2, 1)]
    slots = slot_block.shape[1]
    scales = (grad_scale, mean_scale)
    outs = [((16, 32, 288), F32), ((512, 512), F32), ((16, 32, 32), F32), ((half, slots, 288), F32)]
    halves = [((shape[0] // 2, *shape[1:]), kind) for shape, kind in outs]
    scratch = [pltpu.VMEM((640, 128), F32), pltpu.VMEM((48, half // 2, 288), F32)]
    crossed = [swap(jnp.stack(early), 1, 0)] + [swap(v, 1, 0) for v in late]
    mine = call(
        functools.partial(half_kernel, scales), halves, scratch, slot_block, *early, *late, flops=HALF_FLOPS
    )
    group_grad, proj_grad, out_factor, factor_owned = call(
        functools.partial(finish_kernel, scales),
        outs,
        scratch + [pltpu.VMEM(shape, kind) for shape, kind in halves] + [pltpu.SemaphoreType.DMA((8,))],
        slot_block,
        *mine,
        *crossed,
        out_hbm=True,
    )
    return group_grad.transpose(0, 2, 1), proj_grad, out_factor, factor_owned.transpose(1, 0, 2)


def solution(mesh):
    placed = (P(AXES, None, None, None), P(AXES, None, None, None), P(), P(), P(), P(), P())
    return jax.shard_map(
        functools.partial(per_device, mesh.shape["owner"], mesh.shape["dp"]),
        mesh=mesh,
        in_specs=placed,
        out_specs=(P(), P(), P(), P("owner", "dp", None)),
        check_vma=False,
    )
```
